32 devices in a mesh: dp: 16 (over z, y, core), blk: 2 (over x).
Axes of the slice: x: 2, y: 2, z: 4, core: 2. Of those that a mesh axis runs over, the one named last changes fastest.
Arguments:
- tokens: bfloat16 [64, 1024, 512], P('dp', 'blk'), may hold values from -6 to 6
- seq_counts: int32 [16], P('dp'), may hold values from 2 to 4, as said below
- norm1_gain: float32 [512], replicated, may hold values from 0.1 to 1.9
- w_query: bfloat16 [512, 512], replicated, may hold values from -0.25 to 0.25
- w_key: bfloat16 [512, 512], replicated, may hold values from -0.25 to 0.25
- w_value: bfloat16 [512, 512], replicated, may hold values from -0.25 to 0.25
- output_weight: bfloat16 [512, 512], replicated, may hold values from -1 to 1
- norm2_gain: float32 [512], replicated, may hold values from 0.1 to 1.9
- router_weight: bfloat16 [512, 2], replicated, may hold values from -0.125 to 0.125
- w_expert_in: bfloat16 [2, 512, 2048], replicated, may hold values from -0.75 to 0.75
- w_expert_out: bfloat16 [2, 2048, 512], replicated, may hold values from -0.375 to 0.375
- cotangent: bfloat16 [64, 1024, 512], P('dp', 'blk'), may hold values from -6 to 6
Outputs:
- output: bfloat16 [64, 1024, 512], P('dp', 'blk')
- grad_tokens: bfloat16 [64, 1024, 512], P('dp', 'blk')
- grad_norm1_gain: float32 [512], replicated
- grad_w_query: float32 [512, 512], replicated
- grad_w_key: float32 [512, 512], replicated
- grad_w_value: float32 [512, 512], replicated
- grad_w_out: float32 [512, 512], replicated
- grad_norm2_gain: float32 [512], replicated
- grad_w_router: float32 [512, 2], replicated
- grad_w_expert_in: float32 [2, 512, 2048], replicated
- grad_w_expert_out: float32 [2, 2048, 512], replicated
The draws below stay inside these ranges and needn't reach their ends.
Inputs may be any that keep to these rules, and one draw needn't show every extreme that they name: `seq_counts`: at least one index of dp has all 4 slots live.
All inputs are finite; a program needn't handle non-finite values.
Results may differ from the reference program's by a relative error of at most 0.018.
Values may be sent and summed in bfloat16 or wider, within the bound.
No kernel may reach another device: no remote copies, remote signals or barrier semaphores. Data moves between devices by JAX's collectives and lax.ppermute only.
A program may use at most 320 MiB of HBM per device.

```python
import jax
import jax.numpy as jnp
from jax import lax

D = 512
ATTENTION_HEADS = 8
HEAD_FEATURES = 64
FF = 2048
EXPERTS = 2
SEQ_MAX = 4
SEQUENCE_LENGTH = 1024
SEQS = 64
N_DP = 16


def draw_seq_counts(key, part):
    key = jax.random.fold_in(key, 7)
    first_key, second_key = jax.random.split(key)
    lowest = max(2, SEQ_MAX // 4)
    counts = jax.random.randint(first_key, (N_DP,), lowest, SEQ_MAX + 1)
    chosen = jax.random.randint(second_key, (), 0, N_DP)
    return jnp.where(jnp.arange(N_DP) == chosen, SEQ_MAX, counts).astype(jnp.int32)


def block_scale(rng, shape, cuts, low, high):
    level = 1.0
    for position, parts in cuts:
        draws = jax.random.uniform(jax.random.fold_in(jax.random.fold_in(rng, 6), position), (parts,), jnp.float32, low / len(cuts), high / len(cuts))
        level = level * jnp.repeat(jnp.exp(draws), shape[position] // parts).reshape((-1,) + (1,) * (len(shape) - 1 - position))
    return level


def centred(key, dims, scale, bound, shards=(), kind=jnp.bfloat16):
    values = jax.random.normal(key, dims, jnp.float32) * scale
    if len(shards) > 0:
        values = block_scale(key, dims, shards, -0.22, 0.18) * values
    return jnp.clip(values, min=-bound, max=bound).astype(kind)


def setup_inputs(seed: int = 0) -> dict:
    streams_of = jax.random.split(jax.random.key(seed), 13)
    tokens = centred(streams_of[0], (SEQS, SEQUENCE_LENGTH, D), 1.0, 6.0, ((0, 16), (1, 2)))
    seq_counts = draw_seq_counts(jax.random.fold_in(streams_of[12], 71), 0)
    norm1_gain = jnp.clip(1.0 + 0.18 * jax.random.normal(streams_of[2], (D,), jnp.float32), 0.1, 1.9)
    w_query = centred(streams_of[3], (D, D), D ** -0.5, 0.25)
    w_key = centred(streams_of[4], (D, D), D ** -0.5, 0.25)
    w_value = centred(streams_of[5], (D, D), D ** -0.5, 0.25)
    output_weight = centred(streams_of[6], (D, D), (D // 16) ** -0.5, 1.0)
    norm2_gain = jnp.clip(1.0 + 0.18 * jax.random.normal(streams_of[7], (D,), jnp.float32), 0.1, 1.9)
    router_weight = centred(streams_of[8], (D, EXPERTS), (4 * D) ** -0.5, 0.125)
    w_expert_in = centred(streams_of[9], (EXPERTS, D, FF), (D // 8) ** -0.5, 0.75)
    w_expert_out = centred(streams_of[10], (EXPERTS, FF, D), (FF // 8) ** -0.5, 0.375)
    cotangent = centred(streams_of[11], (SEQS, SEQUENCE_LENGTH, D), 1.0, 6.0, ((0, 16), (1, 2)))
    return {"tokens": tokens, "seq_counts": seq_counts, "norm1_gain": norm1_gain, "w_query": w_query, "w_key": w_key, "w_value": w_value, "output_weight": output_weight, "norm2_gain": norm2_gain, "router_weight": router_weight, "w_expert_in": w_expert_in, "w_expert_out": w_expert_out, "cotangent": cotangent}


@jax.custom_vjp
def low(v):
    return lax.optimization_barrier(v.astype(jnp.bfloat16)).astype(jnp.float32)

@jax.custom_vjp
def lower_backward(v):
    return v

def low_keep(v):
    return (low(v), None)

def low_pass(kept, grad):
    return (grad,)

def back_keep(v):
    return (v, None)

def back_low(kept, grad):
    return (low(grad),)
low.defvjp(low_keep, low_pass)
lower_backward.defvjp(back_keep, back_low)

def lower_combined(value):
    return low(lower_backward(value))

def exact_product(form, left, right):
    return jnp.einsum(form, left, right, precision=lax.Precision.HIGHEST)

def layer_norm(value, gain):
    center = value - lax.optimization_barrier(jnp.mean(value, axis=-1, keepdims=True))
    spread = lax.optimization_barrier(jnp.mean(center * center, axis=-1, keepdims=True))
    return center * lax.rsqrt(spread + 1e-05) * gain

def attend_sequence(pieces):
    query, key_rows, value_rows = pieces
    scores = lower_backward(exact_product('qhd,khd->hqk', query, key_rows)) * HEAD_FEATURES ** (-0.5)
    positions = jnp.arange(SEQUENCE_LENGTH, dtype=jnp.int32)
    allowed = positions[:, None] >= positions[None, :]
    scores = jnp.where(allowed[None], scores, -1e+30)
    powers = jnp.exp(scores - lax.optimization_barrier(jnp.max(scores, axis=-1, keepdims=True)))
    probs = low(powers / lax.optimization_barrier(jnp.sum(powers, axis=-1, keepdims=True)))
    return exact_product('hqk,khd->qhd', probs, value_rows)

def forward(tokens, norm1_gain, w_query, w_key, w_value, output_weight, norm2_gain, router_weight, w_expert_in, w_expert_out, live):
    expert_slots = tokens.shape[0]
    first_half = low(layer_norm(tokens, norm1_gain))

    def project(weight_matrix):
        return lower_combined(exact_product('yrx,xc->yrc', first_half, weight_matrix)).reshape(expert_slots, SEQUENCE_LENGTH, ATTENTION_HEADS, HEAD_FEATURES)
    query = project(w_query)
    key_rows = project(w_key)
    value_rows = project(w_value)
    core_tokens = lax.map(jax.checkpoint(attend_sequence), (query, key_rows, value_rows))
    core_tokens = lower_combined(core_tokens).reshape(expert_slots, SEQUENCE_LENGTH, D)
    residual_stream = tokens + lower_backward(exact_product('yrx,xc->yrc', core_tokens, output_weight))
    second_half = low(layer_norm(residual_stream, norm2_gain))
    router_logits = lower_backward(exact_product('yrx,xc->yrc', second_half, router_weight))
    gate_live = live.astype(tokens.dtype)[:, None, None]
    masked = jnp.where(gate_live > 0, router_logits, -1e+30)
    powers = jnp.exp(masked - lax.optimization_barrier(jnp.max(masked, axis=0, keepdims=True))) * gate_live
    mixing_weights = low(powers / lax.optimization_barrier(jnp.sum(powers, axis=0, keepdims=True)))
    merged_tokens = lower_combined(exact_product('onk,onc->nkc', mixing_weights, second_half))
    hidden = low(jax.nn.gelu(lower_backward(exact_product('led,edf->lef', merged_tokens, w_expert_in))))
    expert_output = lower_combined(exact_product('lef,efd->led', hidden, w_expert_out))
    return residual_stream + exact_product('ufj,fjt->uft', mixing_weights, expert_output)

def reference(tokens, seq_counts, norm1_gain, w_query, w_key, w_value, output_weight, norm2_gain, router_weight, w_expert_in, w_expert_out, cotangent):
    params = (norm1_gain.astype(jnp.float32), w_query.astype(jnp.float32), w_key.astype(jnp.float32), w_value.astype(jnp.float32), output_weight.astype(jnp.float32), norm2_gain.astype(jnp.float32), router_weight.astype(jnp.float32), w_expert_in.astype(jnp.float32), w_expert_out.astype(jnp.float32))
    grouped = tokens.reshape(N_DP, SEQ_MAX, SEQUENCE_LENGTH, D)
    grouped_cot = cotangent.reshape(N_DP, SEQ_MAX, SEQUENCE_LENGTH, D)

    def group_step(running, group_item):
        group_tokens, group_cot, count = group_item
        live = jnp.arange(SEQ_MAX, dtype=jnp.int32) < count

        def layer(values, *weights):
            return forward(values, *weights, live)
        result, pullback = jax.vjp(layer, group_tokens.astype(jnp.float32), *params)
        gradients = pullback(group_cot.astype(jnp.float32))
        running = tuple((so_far + newest for so_far, newest in zip(running, gradients[1:])))
        return (running, (result.astype(jnp.bfloat16), gradients[0].astype(jnp.bfloat16)))
    start = tuple((jnp.zeros_like(weight_matrix) for weight_matrix in params))
    sums, (outputs, input_grads) = lax.scan(group_step, start, (grouped, grouped_cot, seq_counts))
    return (outputs.reshape(SEQS, SEQUENCE_LENGTH, D), input_grads.reshape(SEQS, SEQUENCE_LENGTH, D), sums[0], sums[1], sums[2], sums[3], sums[4], sums[5], sums[6], sums[7], sums[8])
```

```python
import math

import jax
import jax.numpy as jnp
from jax import lax
from jax.experimental import pallas as pl
from jax.experimental.pallas import tpu as pltpu
from jax.sharding import PartitionSpec as P

HEADS = 8
HEAD = 64
PAIR = 2 * HEAD
QUAD = 4 * HEAD
EPS = 1e-05
SCALE = HEAD ** (-0.5)
SCALE2 = SCALE * math.log2(math.e)
TILE = 256
BF = jnp.bfloat16
F32 = jnp.float32
AXES = ("dp", "blk")
MIB = 1 << 20
LIMIT = 60
FLOPS = 2_000_000_000


def dot(left, right):
    return jnp.dot(left, right, preferred_element_type=F32)


def dot_nt(left, right):
    return lax.dot_general(left, right, (((1,), (1,)), ((), ())), preferred_element_type=F32)


def normed(value):
    center = value - jnp.mean(value, axis=-1, keepdims=True)
    inverse = lax.rsqrt(jnp.mean(center * center, axis=-1, keepdims=True) + EPS)
    return center * inverse, inverse


def norm_back(scaled, hat, inverse):
    return inverse * (
        scaled
        - jnp.mean(scaled, axis=-1, keepdims=True)
        - hat * jnp.mean(scaled * hat, axis=-1, keepdims=True)
    )


def lane_masks(dtype):
    lane = lax.broadcasted_iota(jnp.int32, (1, PAIR), 1)
    low = (lane < HEAD).astype(F32)
    return low.astype(dtype), (1.0 - low).astype(dtype)


def causal_tile():
    shape = (TILE, TILE)
    return lax.broadcasted_iota(jnp.int32, shape, 0) <= lax.broadcasted_iota(jnp.int32, shape, 1)


def params(limit, *semantics):
    return pltpu.CompilerParams(
        vmem_limit_bytes=limit * MIB, dimension_semantics=semantics or ("arbitrary",)
    )


def cost(us):
    return pl.CostEstimate(flops=int(us * FLOPS), bytes_accessed=1000, transcendentals=0)


def call(kernel, name, us, grid, inputs, outputs, scratch, deps, place):
    any_ref = pl.BlockSpec(memory_space=pl.ANY)

    def body(place_ref, *refs):
        kernel(place_ref, *refs[len(deps) :])

    return pl.pallas_call(
        body,
        grid_spec=pltpu.PrefetchScalarGridSpec(
            num_scalar_prefetch=1,
            grid=grid,
            in_specs=[any_ref] * len(deps) + [pl.BlockSpec(b, i) for _, b, i in inputs],
            out_specs=[pl.BlockSpec(b, i) for _, _, b, i in outputs],
            scratch_shapes=scratch,
        ),
        out_shape=[jax.ShapeDtypeStruct(shape, kind) for shape, kind, _, _ in outputs],
        compiler_params=params(LIMIT, *["arbitrary"] * len(grid)),
        cost_estimate=cost(us),
        name=name,
    )(place, *deps, *[array for array, _, _ in inputs])


def whole(array):
    zeros = (0,) * array.ndim
    return array, array.shape, lambda *_: zeros


def same(*index):
    return lambda step, *_: index


def forward_kernel(
    place, tok, got, gain, wq, wk, wv, first, query, keys, values, core_own, core_far, stats, core
):
    half = got.shape[0]
    full = 2 * half
    here = pl.multiple_of(place[0] * half, half)
    there = pl.multiple_of((1 - place[0]) * half, half)

    @pl.when(pl.program_id(0) == 0)
    def _():
        first[pl.ds(here, half), :] = (normed(tok[0].astype(F32))[0] * gain[...]).astype(BF)
        first[pl.ds(there, half), :] = (normed(got[...].astype(F32))[0] * gain[...]).astype(BF)

    rows = first[...]
    query[...] = dot(rows, wq[...]).astype(BF)
    keys[...] = dot(rows, wk[...]).astype(BF)
    values[...] = dot(rows, wv[...]).astype(BF)
    masks = lane_masks(BF)
    values_t = values[...].T
    causal = causal_tile()
    tasks = [
        (head, block) for head in range(query.shape[1] // HEAD) for block in range(full // TILE)
    ]

    def score(head, block):
        pair = slice(head // 2 * PAIR, (head // 2 + 1) * PAIR)
        count = (block + 1) * TILE
        key_half = keys[:count, pair] * masks[head % 2]
        return dot_nt(key_half, query[block * TILE : count, pair])

    def soften(head, block, scores):
        count = (block + 1) * TILE
        near = jnp.where(causal, scores[count - TILE :], -1e30)
        if block > 0:
            near = jnp.concatenate([scores[: count - TILE], near], axis=0)
        top = jnp.max(near, axis=0, keepdims=True)
        powers = jnp.exp2((near - top) * SCALE2)
        total = jnp.sum(powers, axis=0, keepdims=True)
        stats[0, head : head + 1, block * TILE : count] = top * SCALE2 + jnp.log2(total)
        return powers.astype(BF), 1.0 / total

    def gather(head, block, powers, share):
        count = (block + 1) * TILE
        lanes = slice(head * HEAD, (head + 1) * HEAD)
        core[lanes, block * TILE : count] = dot(values_t[lanes, :count], powers) * share

    scores = score(*tasks[0])
    waiting = None
    for n, task in enumerate(tasks):
        ahead = score(*tasks[n + 1]) if n + 1 < len(tasks) else None
        softened = soften(*task, scores)
        if waiting is not None:
            gather(*waiting)
        waiting = task + softened
        scores = ahead
    gather(*waiting)
    core_own[...] = core[:, pl.ds(here, half)].T.astype(BF)
    core_far[...] = core[:, pl.ds(there, half)].T.astype(BF)


def attend(index, place, tokens, got, gain, wq, wk, wv):
    _, half, width = tokens.shape
    full = 2 * half
    quads = width // QUAD
    column = ((width, QUAD), lambda p, s: (0, p))
    wide = ((full, width), BF, (full, QUAD), lambda p, s: (0, p))
    part = ((half, width), BF, (half, QUAD), lambda p, s: (0, p))
    return call(
        forward_kernel,
        "attend_forward",
        13,
        (quads,),
        [
            (tokens, (1, half, width), lambda p, s: (2 * s[0] + index, 0, 0)),
            whole(got),
            whole(gain),
            (wq, *column),
            (wk, *column),
            (wv, *column),
        ],
        [
            ((full, width), BF, (full, width), same(0, 0)),
            wide,
            wide,
            wide,
            part,
            part,
            ((quads, 8, full), F32, (1, 8, full), lambda p, s: (p, 0, 0)),
        ],
        [pltpu.VMEM((QUAD, full), F32)],
        [],
        place,
    )


def mix_kernel(place, tok, cot, c0, c1, c2, c3, wo, gain, router, resid, merged, d_expert, gates):
    slots, rows, width = tok.shape
    attended = dot(jnp.concatenate([c0[...], c1[...], c2[...], c3[...]], axis=0), wo[...])
    seconds, logits, lives = [], [], []
    for r in range(slots):
        slot = lax.rem(r + 2 * place[0], slots)
        stream = tok[slot].astype(F32) + attended[r * rows : (r + 1) * rows]
        resid[r] = stream
        second = (normed(stream)[0] * gain[...]).astype(BF)
        seconds.append(second.astype(F32))
        live = slot < place[1]
        lives.append(live)
        logits.append(jnp.where(live, dot(second, router[...]), -1e30))
    top = jnp.maximum(jnp.maximum(logits[0], logits[1]), jnp.maximum(logits[2], logits[3]))
    powers = [jnp.where(lives[r], jnp.exp(logits[r] - top), 0.0) for r in range(slots)]
    total = powers[0] + powers[1] + powers[2] + powers[3]
    weights = []
    for r in range(slots):
        gate = powers[r] / total
        gates[r] = gate
        weights.append(gate.astype(BF).astype(F32))
    for e in range(2):
        both = jnp.zeros((rows, width), F32)
        back = jnp.zeros((rows, width), F32)
        for r in range(slots):
            slot = lax.rem(r + 2 * place[0], slots)
            weight = weights[r][:, e : e + 1]
            both = both + weight * seconds[r]
            back = back + weight * cot[slot].astype(F32)
        merged[e] = both.astype(BF)
        d_expert[e] = back.astype(BF)


def mix(place, tokens, cotangent, cores, output_weight, gain, router):
    slots, half, width = tokens.shape
    rows = 128
    quad = ((slots, rows, width), lambda p, s: (0, p, 0))
    part = ((rows, width), lambda p, s: (p, 0))
    twin = ((2, half, width), BF, (2, rows, width), lambda p, s: (0, p, 0))
    return call(
        mix_kernel,
        "mix",
        9,
        (half // rows,),
        [(tokens, *quad), (cotangent, *quad)]
        + [(core, *part) for core in cores]
        + [whole(output_weight), whole(gain), whole(router)],
        [
            ((slots, half, width), F32, *quad),
            twin,
            twin,
            ((slots, half, 128), F32, (slots, rows, 128), lambda p, s: (0, p, 0)),
        ],
        [],
        [],
        place,
    )


def expert_kernel(
    per, place, merged, d_expert, w_in, w_out, out, d_merged, keep, give, acc, d_acc, rows_t
):
    step = pl.program_id(0)
    rows = merged[0]
    back = d_expert[0]
    width = back.shape[1]
    root = math.sqrt(2.0 / math.pi)
    parts = w_in.shape[2] // TILE
    many = width // per
    mine = place[2] == 0

    @pl.when(step == 0)
    def _():
        rows_t[...] = rows.T

    def spans(n):
        return slice(n * TILE, (n + 1) * TILE)

    def ahead(n):
        return dot(rows, w_in[0, :, spans(n)]), dot_nt(back, w_out[0, spans(n), :])

    def bend(u, d_hidden):
        square = u * u
        bent = jnp.tanh(u * (root + (root * 0.044715) * square))
        hidden = (0.5 * u * (1.0 + bent)).astype(BF)
        slope = 0.5 * (1.0 + bent) + (0.5 * u) * (1.0 - bent * bent) * (
            root + (3.0 * root * 0.044715) * square
        )
        return hidden, (d_hidden * slope).astype(BF)

    def spread(n, hidden, d_pre):
        to_out = dot(hidden.T, back)
        to_out = jnp.concatenate([to_out[:, :TILE], to_out[:, TILE:]], axis=0)
        to_in = dot(rows_t[...], d_pre)
        shape = (many, per, TILE)
        at = slice(n * many, (n + 1) * many)
        keep[at] = jnp.where(mine, to_in, to_out).astype(BF).reshape(shape)
        give[at] = jnp.where(mine, to_out, to_in).astype(BF).reshape(shape)
        return dot(hidden, w_out[0, spans(n), :]), dot_nt(d_pre, w_in[0, :, spans(n)])

    forth, down, waiting = 0.0, 0.0, None
    current = ahead(0)
    for n in range(parts):
        later = ahead(n + 1) if n + 1 < parts else None
        bent = bend(*current)
        if waiting is not None:
            pair = spread(*waiting)
            forth, down = forth + pair[0], down + pair[1]
        waiting = (n,) + bent
        current = later
    pair = spread(*waiting)
    forth, down = forth + pair[0], down + pair[1]

    @pl.when(step == 0)
    def _():
        acc[...] = forth
        d_acc[...] = down

    @pl.when(step == pl.num_programs(0) - 1)
    def _():
        out[...] = (acc[...] + forth).astype(BF)
        d_merged[...] = (d_acc[...] + down).astype(BF)


def expert(e, place, count, merged, d_expert, w_in, w_out, deps):
    _, rows, width = merged.shape
    hidden = w_in.shape[2]
    chunk = hidden // 2
    per = hidden // TILE * width // count
    one = ((1, rows, width), same(e, 0, 0))
    flat = ((rows, width), BF, (rows, width), same(0, 0))
    part = ((count, per, TILE), BF, (count // 2, per, TILE), lambda f, s: (f, 0, 0))
    return call(
        lambda *refs: expert_kernel(per, *refs),
        "expert",
        13,
        (2,),
        [
            (merged, *one),
            (d_expert, *one),
            (w_in, (1, width, chunk), lambda f, s: (e, 0, f)),
            (w_out, (1, chunk, width), lambda f, s: (e, f, 0)),
        ],
        [flat, flat, part, part],
        [
            pltpu.VMEM((rows, width), F32),
            pltpu.VMEM((rows, width), F32),
            pltpu.VMEM((width, rows), BF),
        ],
        deps,
        place,
    )


def low_kernel(
    place, resid, cot, gates, x0, x1, m0, m1, router, gain, d2, d3, d0, lows_out, g_router, g_gain
):
    slots, rows, width = resid.shape
    outs = [x0[...].astype(F32), x1[...].astype(F32)]
    downs = [m0[...].astype(F32), m1[...].astype(F32)]
    lane = lax.broadcasted_iota(jnp.int32, (rows, 128), 1)
    hats, inverses, seconds, d_gates = [], [], [], []
    for r in range(slots):
        slot = lax.rem(r + 2 * place[0], slots)
        hat, inverse = normed(resid[r])
        second = (hat * gain[...]).astype(BF)
        hats.append(hat)
        inverses.append(inverse)
        seconds.append(second)
        cotangent = cot[slot].astype(F32)
        second = second.astype(F32)
        columns = [
            jnp.sum(cotangent * outs[e] + downs[e] * second, axis=-1, keepdims=True)
            for e in range(2)
        ]
        d_gates.append(jnp.where(lane == 0, columns[0], jnp.where(lane == 1, columns[1], 0.0)))
    mean = sum(gates[r] * d_gates[r] for r in range(slots))
    lows = [(gates[r] * (d_gates[r] - mean)).astype(BF) for r in range(slots)]
    gain_sum = jnp.zeros((1, width), F32)
    for r in range(slots):
        low = lows[r].astype(F32)
        lows_out[r] = low
        if r != 1:
            d_rows, gain_part = resid_back(
                cot[lax.rem(r + 2 * place[0], slots)], gates[r], low, downs, router, gain,
                hats[r], inverses[r],
            )
            {2: d2, 3: d3, 0: d0}[r][...] = d_rows
            gain_sum = gain_sum + gain_part
    low_rows = jnp.concatenate(lows, axis=0).astype(F32).T[:8].astype(BF)
    router_sum = dot(low_rows, jnp.concatenate(seconds, axis=0))
    add_up(g_router, router_sum)
    add_up(g_gain, jnp.broadcast_to(gain_sum, (8, width)))


def add_up(ref, value):
    @pl.when(pl.program_id(0) == 0)
    def _():
        ref[...] = value

    @pl.when(pl.program_id(0) > 0)
    def _():
        ref[...] += value


def resid_back(cotangent, gate, low, downs, router, gain, hat, inverse):
    weight = gate.astype(BF).astype(F32)
    d_second = sum(
        weight[:, e : e + 1] * downs[e] + low[:, e : e + 1] * router[e : e + 1, :]
        for e in range(2)
    )
    d_stream = norm_back(d_second * gain[...], hat, inverse)
    d_rows = (cotangent.astype(F32) + d_stream).astype(BF)
    return d_rows, jnp.sum(d_second * hat, axis=0, keepdims=True)


def own_kernel(
    place, resid, cot, gates, lows, m0, m1, router, gain, c0, c1, c2, c3, d0, d2, d3, g_router,
    g_gain_far, d1, keep, give, g_gain, g_out,
):
    step = pl.program_id(0)
    width = resid.shape[2]
    downs = [m0[...].astype(F32), m1[...].astype(F32)]
    hat, inverse = normed(resid[0])
    d_rows, gain_part = resid_back(
        cot[0], gates[0], lows[0], downs, router, gain, hat, inverse
    )
    d1[...] = d_rows
    add_up(g_gain, jnp.broadcast_to(gain_part, (8, width)))
    cores = jnp.concatenate([c0[...], c1[...], c2[...], c3[...]], axis=0)
    rows = jnp.concatenate([d0[...], d_rows, d2[...], d3[...]], axis=0)
    total = dot(cores.T, rows)

    add_up(g_out, total)

    @pl.when(step == pl.num_programs(0) - 1)
    def _():
        mine = place[2] == 0
        low, high = g_out[:, :TILE], g_out[:, TILE:]
        line = lax.broadcasted_iota(jnp.int32, (8, width), 0)
        small = jnp.where(line < 2, g_router[...], 0.0)
        small = jnp.where(line == 2, g_gain_far[...] + g_gain[...], small)
        small = jnp.concatenate(
            [small[:, :TILE], small[:, TILE:], jnp.zeros((width - 16, TILE), F32)], axis=0
        )
        blank = jnp.zeros((width, TILE), F32)
        one = jnp.concatenate([jnp.where(mine, low, high), jnp.where(mine, small, blank)])
        two = jnp.concatenate([jnp.where(mine, high, low), jnp.where(mine, blank, small)])
        keep[...] = one.astype(BF)
        give[...] = two.astype(BF)


def output_kernel(place, resid, gates, x0, x1, output):
    slots = resid.shape[0]
    outs = [x0[...].astype(F32), x1[...].astype(F32)]
    for r in range(slots):
        slot = lax.rem(r + 2 * place[0], slots)
        weight = gates[r].astype(BF).astype(F32)
        output[slot] = (
            resid[r] + weight[:, 0:1] * outs[0] + weight[:, 1:2] * outs[1]
        ).astype(BF)


def blocks_of(slots, rows, width):
    return dict(
        quad=((slots, rows, width), lambda p, s: (0, p, 0)),
        other=((1, rows, width), lambda p, s: (1, p, 0)),
        our_other=((1, rows, width), lambda p, s: (2 * s[0] + 1, p, 0)),
        other_lanes=((1, rows, 128), lambda p, s: (1, p, 0)),
        lanes=((slots, rows, 128), lambda p, s: (0, p, 0)),
        part=((rows, width), lambda p, s: (p, 0)),
        eight=((8, width), same(0, 0)),
    )


def unmix_far(place, resid, cotangent, gates, outs, downs, router, gain, deps):
    slots, half, width = resid.shape
    b = blocks_of(slots, 128, width)
    return call(
        low_kernel,
        "unmix_far",
        9,
        (half // 128,),
        [(resid, *b["quad"]), (cotangent, *b["quad"]), (gates, *b["lanes"])]
        + [(value, *b["part"]) for value in (*outs, *downs)]
        + [whole(router), whole(gain)],
        [((half, width), BF, *b["part"])] * 3
        + [((slots, half, 128), F32, *b["lanes"])]
        + [((8, width), F32, *b["eight"])] * 2,
        [],
        deps,
        place,
    )


def unmix_own(
    place, resid, cotangent, gates, lows, downs, router, gain, cores, d_rows, g_router, gain_far, deps
):
    slots, half, width = resid.shape
    b = blocks_of(slots, 128, width)
    rest = ((2 * width, TILE), BF, (2 * width, TILE), same(0, 0))
    return call(
        own_kernel,
        "unmix_own",
        8,
        (half // 128,),
        [(resid, *b["other"]), (cotangent, *b["our_other"])]
        + [(value, *b["other_lanes"]) for value in (gates, lows)]
        + [(value, *b["part"]) for value in downs]
        + [whole(router), whole(gain)]
        + [(value, *b["part"]) for value in (*cores, *d_rows)]
        + [whole(g_router), whole(gain_far)],
        [((half, width), BF, *b["part"]), rest, rest],
        [pltpu.VMEM((8, width), F32), pltpu.VMEM((width, width), F32)],
        deps,
        place,
    )


def write_output(place, resid, gates, outs, deps):
    slots, half, width = resid.shape
    b = blocks_of(slots, 128, width)
    return call(
        output_kernel,
        "write_output",
        6,
        (half // 128,),
        [(resid, *b["quad"]), (gates, *b["lanes"])] + [(value, *b["part"]) for value in outs],
        [((slots, half, width), BF, *b["quad"])],
        [],
        deps,
        place,
    )[0]


def backward_kernel(
    place, d_own, d_got, query, keys, values, core_own, core_far, stats, wo, three,
    d_attn, core, dq_t, d_keys, d_values,
):
    half = d_own.shape[0]
    full = 2 * half
    here = pl.multiple_of(place[0] * half, half)
    there = pl.multiple_of((1 - place[0]) * half, half)
    d_attn[pl.ds(here, half), :] = d_own[...]
    d_attn[pl.ds(there, half), :] = d_got[...]
    core[pl.ds(here, half), :] = core_own[...]
    core[pl.ds(there, half), :] = core_far[...]
    d_core = dot_nt(d_attn[...], wo[...]).astype(BF)
    product = (d_core.astype(F32) * core[...].astype(F32)).T
    masks = lane_masks(BF)
    keys_t = keys[...].T
    causal = causal_tile()
    tasks = [
        (head, block) for head in range(query.shape[1] // HEAD) for block in range(full // TILE)
    ]

    def of_pair(head):
        return slice(head // 2 * PAIR, (head // 2 + 1) * PAIR)

    def score(head, block):
        pair, mask, count = of_pair(head), masks[head % 2], (block + 1) * TILE
        span = slice(block * TILE, count)
        scores = dot_nt(keys[:count, pair] * mask, query[span, pair])
        d_probs = dot_nt(values[:count, pair] * mask, d_core[span, pair])
        return scores, d_probs

    def soften(head, block, scores, d_probs):
        count = (block + 1) * TILE
        span = slice(block * TILE, count)
        delta = jnp.sum(product[head * HEAD : (head + 1) * HEAD, span], axis=0, keepdims=True)
        probs = jnp.exp2(scores * SCALE2 - stats[0, head : head + 1, span])
        near = jnp.where(causal, probs[count - TILE :], 0.0)
        if block > 0:
            near = jnp.concatenate([probs[: count - TILE], near], axis=0)
        return near.astype(BF), (near * (d_probs - delta)).astype(BF)

    def spread(head, block, probs, d_scores):
        pair, mask, count = of_pair(head), masks[head % 2], (block + 1) * TILE
        span, before = slice(block * TILE, count), slice(0, count - TILE)
        lanes = slice(head * HEAD, (head + 1) * HEAD)
        to_value = dot(probs, d_core[span, pair] * mask)
        to_key = dot(d_scores, query[span, pair] * mask)
        if head % 2 == 0:
            d_values[span, pair] = to_value[count - TILE :]
            d_keys[span, pair] = to_key[count - TILE :]
            if block > 0:
                d_values[before, pair] += to_value[before]
                d_keys[before, pair] += to_key[before]
        else:
            d_values[:count, pair] += to_value
            d_keys[:count, pair] += to_key
        dq_t[lanes, span] = dot(keys_t[lanes, :count], d_scores)

    scored = score(*tasks[0])
    waiting = None
    for n, task in enumerate(tasks):
        ahead = score(*tasks[n + 1]) if n + 1 < len(tasks) else None
        softened = soften(*task, *scored)
        if waiting is not None:
            spread(*waiting)
        waiting = task + softened
        scored = ahead
    spread(*waiting)
    three[:, :QUAD] = (dq_t[...].T * SCALE).astype(BF)
    three[:, QUAD : 2 * QUAD] = (d_keys[...] * SCALE).astype(BF)
    three[:, 2 * QUAD :] = d_values[...].astype(BF)


def attend_back(quad, place, d_own, d_got, kept, wo, deps):
    first, query, keys, values, core_own, core_far, stats = kept
    half, width = d_own.shape
    full = 2 * half
    wide = ((full, QUAD), same(0, quad))
    part = ((half, QUAD), same(0, quad))
    return call(
        backward_kernel,
        "attend_backward",
        11,
        (1,),
        [
            whole(d_own),
            whole(d_got),
            (query, *wide),
            (keys, *wide),
            (values, *wide),
            (core_own, *part),
            (core_far, *part),
            (stats, (1, 8, full), same(quad, 0, 0)),
            (wo, (QUAD, width), same(quad, 0)),
        ],
        [((full, 3 * QUAD), BF, (full, 3 * QUAD), same(0, 0))],
        [
            pltpu.VMEM((full, width), BF),
            pltpu.VMEM((full, QUAD), BF),
            pltpu.VMEM((QUAD, full), F32),
            pltpu.VMEM((full, QUAD), F32),
            pltpu.VMEM((full, QUAD), F32),
        ],
        deps,
        place,
    )


def first_kernel(place, t0, t1, own, got, gain, wq, wk, wv, d_tok_own, d_tok_far):
    d_first = 0.0
    for quad, three in enumerate((t0, t1)):
        lanes = slice(quad * QUAD, (quad + 1) * QUAD)
        weights = [w[:, lanes] for w in (wq, wk, wv)]
        d_first = d_first + dot_nt(three[...], jnp.concatenate(weights, axis=1))
    near = pl.program_id(0) == 0
    value = jnp.where(near, own[0].astype(F32), got[...].astype(F32))
    hat, inverse = normed(value)
    result = norm_back(d_first * gain[...], hat, inverse).astype(BF)

    @pl.when(near)
    def _():
        d_tok_own[...] = result

    @pl.when(jnp.logical_not(near))
    def _():
        d_tok_far[...] = result


def first_back(index, place, threes, tokens, got, gain, weights, deps):
    _, half, width = tokens.shape
    rows = 256
    blocks = half // rows

    def row_block(h, j, s):
        return (jnp.where(h == 0, s[0], 1 - s[0]) * blocks + j, 0)

    return call(
        first_kernel,
        "first_back",
        6,
        (2, blocks),
        [(three, (rows, three.shape[1]), row_block) for three in threes]
        + [
            (
                tokens,
                (1, rows, width),
                lambda h, j, s: (2 * s[0] + index, jnp.where(h == 0, j, blocks - 1), 0),
            ),
            (got, (rows, width), lambda h, j, s: (jnp.where(h == 0, 0, j), 0)),
            whole(gain),
            *[whole(weight) for weight in weights],
        ],
        [
            (
                (half, width),
                BF,
                (rows, width),
                lambda h, j, s: (jnp.where(h == 0, j, blocks - 1), 0),
            ),
            ((half, width), BF, (rows, width), lambda h, j, s: (jnp.where(h == 0, 0, j), 0)),
        ],
        [],
        deps,
        place,
    )


def project_kernel(place, f0, f1, a0, a1, b0, b1, keep, give, t0, t1):
    @pl.when(pl.program_id(0) == 0)
    def _():
        t0[...] = f0[...].T
        t1[...] = f1[...].T

    mine = place[2] == 0
    low = dot(t0[...], a0[...]) + dot(t1[...], b0[...])
    high = dot(t0[...], a1[...]) + dot(t1[...], b1[...])
    keep[...] = jnp.where(mine, low, high).astype(BF)
    give[...] = jnp.where(mine, high, low).astype(BF)


def project_grads(place, firsts, threes, deps):
    full, width = firsts[0].shape
    column = ((full, QUAD), lambda p, s: (0, p))
    out = ((3 * width, QUAD), BF, (width, QUAD), lambda p, s: (p, 0))
    return call(
        project_kernel,
        "project_grads",
        7,
        (3,),
        [whole(first) for first in firsts]
        + [(three, *column) for pair in threes for three in pair],
        [out, out],
        [pltpu.VMEM((width, full), BF), pltpu.VMEM((width, full), BF)],
        deps,
        place,
    )


def chip_bits(devices):
    return [1] + [1 << n for n in range(2, devices.bit_length() - 1)]


def masks_of(level):
    return [level[0], level[1], level[0] + level[1]] if len(level) > 1 else [level[0]]


def send(value, mask, devices):
    return lax.ppermute(value, AXES, [(n, n ^ mask) for n in range(devices)])


class Summed:
    def __init__(self, lanes, devices, levels, joint):
        self.devices, self.levels, self.joint, self.steps = devices, levels, joint, 0
        self.own, self.count = len(levels[0]), len(levels[0]) + len(joint)
        self.lanes = [
            [[keep, send(give, 2, devices)] for keep, give in lane] for lane in lanes
        ]
        self.rows = [sum(keep.shape[1] for keep, _ in lane) for lane in lanes]

    def masks(self, n):
        if n >= self.own:
            return [masks_of(self.joint[n - self.own])]
        return [masks_of(levels[n]) for levels in self.levels]

    def jobs(self):
        n = self.steps
        if n < self.own:
            return [(lane, levels[n], None) for lane, levels in zip(self.lanes, self.levels)]
        together = [array for lane in self.lanes for array in lane]
        if n <= self.count:
            return [(together, self.joint[n - self.own] if n < self.count else [], None)]
        if 2 * self.count - n == self.own and self.joint:
            return [(lane, None, self.rows) for lane in self.lanes]
        return [(lane, None, [lane[0][0].shape[1]]) for lane in self.lanes]

    def take(self, results):
        n = self.steps
        if n >= self.count:
            results = [[value] for result in results for value in result]
        masks = self.masks(n if n < self.count else 2 * self.count - 1 - n)
        self.lanes = []
        for (mine, *others), some in zip(results, masks):
            if n >= self.count:
                others = [mine] * len(some)
            got = [send(other, mask, self.devices) for other, mask in zip(others, some)]
            self.lanes.append([[mine] + got])
        self.steps += 1

    def done(self):
        return self.steps >= 2 * self.count

    def finish(self):
        parts = [lane[0] for lane in self.lanes]
        return [some + [send(part, 2, self.devices) for part in some] for some in parts]


def step_kernel(kinds, place, *refs):
    ins = sum(sum(groups) for _, groups, _ in kinds)
    inputs, outputs = refs[:ins], refs[ins:]
    for adds, groups, n_out in kinds:
        here, inputs = inputs[: sum(groups)], inputs[sum(groups) :]
        there, outputs = outputs[:n_out], outputs[n_out:]
        if not adds:
            size, row = here[0].shape[0], 0
            for target in there:
                rows = target.shape[1]
                for n, ref in enumerate(here):
                    target[n * size : (n + 1) * size] = ref[:, row : row + rows, :]
                row += rows
            continue
        for target in there:
            row = 0
            for each in groups[: len(groups) // n_out]:
                total = here[0][...].astype(F32)
                for other in here[1:each]:
                    total = total + other[...].astype(F32)
                here, rows = here[each:], total.shape[1]
                target[:, row : row + rows, :] = total.astype(BF)
                row += rows


def advance(chains, place, deps):
    jobs = [chain.jobs() for chain in chains]
    every = [job for some in jobs for job in some]
    splits = [arrays[0][0].shape[0] >> len(level or []) for arrays, level, _ in every]
    big = max(array[0].size for arrays, _, _ in every for array in arrays)
    steps = max(1, 2 * big // MIB) if all(level is not None for _, level, _ in every) else 1
    steps = min([steps] + splits)
    inputs, outputs, kinds = [], [], []
    for (arrays, level, parts), split in zip(every, splits):
        width = arrays[0][0].shape[2]
        if level is None:
            count = split * len(arrays[0])
            inputs += [whole(array) for array in arrays[0]]
            for rows in parts:
                shape = (count, rows, width)
                outputs.append((shape, BF, shape, lambda p, s: (0, 0, 0)))
            kinds.append((False, [len(arrays[0])], len(parts)))
            continue
        block = split // steps
        rows = sum(some[0].shape[1] for some in arrays)

        def index(d, level=level):
            def at(p, s):
                own = 0
                for n, bit in enumerate(level):
                    own = own + (lax.rem(s[4] // bit, 2) << n)
                return ((own ^ d) * steps + p, 0, 0)

            return at

        for d in range(1 << len(level)):
            for some in arrays:
                inputs += [(a, (block,) + a.shape[1:], index(d)) for a in some]
            outputs.append(
                ((split, rows, width), BF, (block, rows, width), lambda p, s: (p, 0, 0))
            )
        n_out = 1 << len(level)
        kinds.append((True, [len(some) for some in arrays] * n_out, n_out))
    results = call(
        lambda *refs: step_kernel(kinds, *refs), "sum_step", 3, (steps,), inputs, outputs, [],
        deps, place,
    )
    mark, groups = results[0], []
    for _, _, n_out in kinds:
        groups.append(results[:n_out])
        results = results[n_out:]
    for chain, some in zip(chains, jobs):
        chain.take(groups[: len(some)])
        groups = groups[len(some) :]
    return [mark]


def result_kernel(per, each, place, own, other, grad_in, grad_out):
    mine = place[2] == 0
    swap = place[3] & (each - 1)
    half = each // 2
    for t in range(each):
        first, second = own[t ^ swap].astype(F32), other[t ^ swap].astype(F32)
        low, high = jnp.where(mine, first, second), jnp.where(mine, second, first)
        grad_in[0, t * per : (t + 1) * per, :] = low
        lanes = slice(t // half * TILE, (t // half + 1) * TILE)
        grad_out[0, t % half * per : (t % half + 1) * per, lanes] = high


def expert_result(e, d, place, chip, own, other, width, hidden, earlier, deps):
    inner, per, _ = own.shape
    each = width // per
    blocks = inner // each
    place = place.at[3].set(chip)

    def piece(k, s):
        return (d ^ (s[3] // inner)) * blocks + k

    part = ((each, per, TILE), lambda k, s: (k ^ ((s[3] % inner) // each), 0, 0))
    inputs = [(own, *part), (other, *part)]
    outputs = [
        ((2, width, hidden), F32, (1, width, TILE), lambda k, s: (e, 0, piece(k, s))),
        ((2, hidden, width), F32, (1, TILE, width), lambda k, s: (e, piece(k, s), 0)),
    ]
    any_ref = pl.BlockSpec(memory_space=pl.ANY)
    held = len(earlier) + len(deps)

    def body(place_ref, *refs):
        result_kernel(per, each, place_ref, *refs[held:])

    return pl.pallas_call(
        body,
        grid_spec=pltpu.PrefetchScalarGridSpec(
            num_scalar_prefetch=1,
            grid=(blocks,),
            in_specs=[any_ref] * held + [pl.BlockSpec(b, i) for _, b, i in inputs],
            out_specs=[pl.BlockSpec(b, i) for _, _, b, i in outputs],
        ),
        out_shape=[jax.ShapeDtypeStruct(shape, kind) for shape, kind, _, _ in outputs],
        input_output_aliases={1 + n: n for n in range(len(earlier))},
        compiler_params=params(LIMIT),
        cost_estimate=cost(4),
        name="expert_result",
    )(place, *earlier, *deps, *[array for array, _, _ in inputs])


def project_result_kernel(place, *refs):
    count = (len(refs) - 11) // 2
    parts, others = refs[:count], refs[count : 2 * count]
    weights, gain = refs[2 * count : 2 * count + 3], refs[2 * count + 3]
    grads, g_gain, small, halves, rest = refs[2 * count + 4 : -4], *refs[-4:]
    inner, rows, _ = parts[0].shape
    width = gain.shape[1]
    per = 3 * width // (count * inner)
    for d in range(count):
        for m in range(inner):
            shard = (d * inner + m) ^ place[3]
            at = pl.ds(pl.multiple_of(shard * per, 8), per)
            more = pl.ds(pl.multiple_of(shard * (rows - per), 8), rows - per)
            for half, source in ((place[2], parts), (1 - place[2], others)):
                value = source[d][m].astype(F32)
                halves[half, at, :] = value[:per]
                rest[half, more, :] = value[per:]
    total = jnp.zeros((width, 1), F32)
    for n in range(4):
        for h in range(2):
            lanes = slice(h * QUAD, (h + 1) * QUAD)
            if n == 3:
                grads[n][:, lanes] = rest[h, :width, :]
                continue
            value = halves[h, n * width : (n + 1) * width, :]
            grads[n][:, lanes] = value
            total += jnp.sum(value * weights[n][:, lanes].astype(F32), axis=1, keepdims=True)
    g_gain[...] = jnp.broadcast_to(total, (width, 128)).T[:8] / gain[...]
    small[:, :QUAD] = rest[0, width : width + 8, :]
    small[:, QUAD:] = rest[0, width + 8 : width + 16, :]


def project_result(place, chip, parts, weights, gain, deps):
    width = gain.shape[1]
    square = ((width, width), F32, (width, width), same(0, 0))
    eight = ((8, width), F32, (8, width), same(0, 0))
    return call(
        project_result_kernel,
        "project_result",
        5,
        (1,),
        [whole(value) for value in (*parts, *weights, gain)],
        [square] * 4 + [eight, eight],
        [pltpu.VMEM((2, 3 * width, QUAD), F32), pltpu.VMEM((2, 2 * width, QUAD), F32)],
        deps,
        place.at[3].set(chip),
    )


def shards(
    tokens, seq_counts, norm1_gain, w_query, w_key, w_value, output_weight, norm2_gain,
    router_weight, w_expert_in, w_expert_out, cotangent,
):
    slots, half, width = tokens.shape
    hidden = w_expert_in.shape[2]
    devices = lax.axis_size("dp") * lax.axis_size("blk")
    count = devices // 2
    blk = lax.axis_index("blk")
    dp = lax.axis_index("dp")
    me = dp * 2 + blk
    core_bit = lax.rem(dp, 2)
    bits = chip_bits(devices)
    x, y, *more = bits
    joint = [[bit] for bit in more]
    lanes = [[[y], [x]], [[x], [y]]]
    levels = [bits[n : n + 2] for n in range(0, len(bits), 2)]

    def chip_of(levels):
        chip = jnp.int32(0)
        for level in levels:
            for bit in reversed(level):
                chip = chip * 2 + lax.rem(me // bit, 2)
        return chip

    place = jnp.stack([blk, seq_counts[0], core_bit, jnp.int32(0), me]).astype(jnp.int32)
    gain1 = norm1_gain.reshape(1, width)
    gain2 = norm2_gain.reshape(1, width)
    router = jnp.pad(router_weight, ((0, 0), (0, 126)))
    router_rows = jnp.pad(router_weight.T.astype(F32), ((0, 6), (0, 0)))
    weights = (w_query, w_key, w_value)

    def swap(value):
        return send(value, 1, devices)

    far = [
        lax.dynamic_index_in_dim(tokens, lax.rem(2 + i + 2 * blk, 4), 0, keepdims=False)
        for i in range(2)
    ]
    got = [swap(value) for value in far]
    kept = [
        attend(i, place, tokens, got[i], gain1, w_query, w_key, w_value) for i in range(2)
    ]
    cores = [kept[0][4], kept[1][4], swap(kept[0][5]), swap(kept[1][5])]
    resid, merged, d_expert, gates = mix(
        place, tokens, cotangent, cores, output_weight, gain2, router
    )
    per = hidden // TILE * width // count
    done = [expert(0, place, count, merged, d_expert, w_expert_in, w_expert_out, [])]
    done.append(
        expert(1, place, count, merged, d_expert, w_expert_in, w_expert_out, [done[0][0]])
    )
    outs, downs = [d[0] for d in done], [d[1] for d in done]
    summed = Summed([[done[0][2:4]], [done[1][2:4]]], devices, lanes, joint)
    d2, d3, d0, lows, g_router, gain_far = unmix_far(
        place, resid, cotangent, gates, outs, downs, router_rows, gain2, []
    )
    d_got = [swap(d2), swap(d3)]
    marks = advance([summed], place, [d2])

    def back(index, quad, deps):
        return attend_back(
            quad, place, d_own[index], d_got[index], kept[index], output_weight, deps
        )[0]

    d_own = [d0, None]
    a0 = back(0, 0, marks)
    d1, *rest = unmix_own(
        place, resid, cotangent, gates, lows, downs, router_rows, gain2, cores, [d0, d2, d3],
        g_router, gain_far, [a0],
    )
    d_own[1] = d1
    rest = [value.reshape(count, -1, TILE) for value in rest]
    a1 = back(0, 1, [d1, d_got[1]])
    far_a = first_back(0, place, [a0, a1], tokens, got[0], gain1, weights, [])
    t_far = [swap(far_a[1])]
    b0 = back(1, 0, advance([summed], place, [far_a[0]]))
    b1 = back(1, 1, [t_far[0]] + advance([summed], place, [b0]))
    pair = project_grads(
        place, [kept[0][0], kept[1][0]], [[a0, a1], [b0, b1]], advance([summed], place, [b1])
    )
    pair = [value.reshape(count, -1, QUAD) for value in pair]
    last = Summed([[pair, rest]], devices, [[]], levels)
    marks = advance([summed], place, [pair[0]])
    marks = advance([last], place, marks)
    far_b = first_back(1, place, [b0, b1], tokens, got[1], gain1, weights, marks)
    t_far.append(swap(far_b[1]))
    marks = advance([summed, last], place, [far_b[0]])
    output = write_output(place, resid, gates, outs, marks)
    marks = advance([summed, last], place, [output, t_far[1]])
    while not (summed.done() and last.done()):
        marks = advance([c for c in (summed, last) if not c.done()], place, marks)
    own = [
        (d.astype(F32) + t.astype(F32)).astype(BF)
        for d, t in zip((d0, d1), (far_a[0], far_b[0]))
    ]
    other = [(d.astype(F32) + t.astype(F32)).astype(BF) for d, t in zip((d2, d3), t_far)]
    grad_tokens = jnp.where(blk == 0, jnp.stack(own + other), jnp.stack(other + own))
    parts = summed.finish()
    results = []
    for d in range(2):
        for e in range(2):
            results = expert_result(
                e, d, place, chip_of(lanes[e] + joint), parts[e][d], parts[e][2 + d], width,
                hidden, results, [],
            )
        if d == 0:
            *grads, grad_gain1, small = project_result(
                place, chip_of(levels), last.finish()[0], weights, gain1, [results[0]]
            )
    grad_in, grad_out = results
    return (
        output, grad_tokens, grad_gain1[0], *grads, small[2], small[:2].T, grad_in, grad_out,
    )


def solution(mesh):
    data = P("dp", "blk", None)
    return jax.shard_map(
        shards,
        mesh=mesh,
        in_specs=(data, P("dp")) + (P(),) * 9 + (data,),
        out_specs=(data, data) + (P(),) * 9,
        check_vma=False,
    )
```

```python
import math

import jax
import jax.numpy as jnp
from jax import lax
from jax.experimental import pallas as pl
from jax.experimental.pallas import tpu as pltpu
from jax.sharding import PartitionSpec as P

HEADS = 8
HEAD = 64
PAIR = 2 * HEAD
QUAD = 4 * HEAD
EPS = 1e-05
SCALE = HEAD ** (-0.5)
SCALE2 = SCALE * math.log2(math.e)
TILE = 256
BF = jnp.bfloat16
F32 = jnp.float32
AXES = ("dp", "blk")
MIB = 1 << 20
LIMIT = 60
FLOPS = 2_000_000_000


def dot(left, right):
    return jnp.dot(left, right, preferred_element_type=F32)


def dot_nt(left, right):
    return lax.dot_general(left, right, (((1,), (1,)), ((), ())), preferred_element_type=F32)


def normed(value):
    center = value - jnp.mean(value, axis=-1, keepdims=True)
    inverse = lax.rsqrt(jnp.mean(center * center, axis=-1, keepdims=True) + EPS)
    return center * inverse, inverse


def norm_back(scaled, hat, inverse):
    return inverse * (
        scaled
        - jnp.mean(scaled, axis=-1, keepdims=True)
        - hat * jnp.mean(scaled * hat, axis=-1, keepdims=True)
    )


def lane_masks(dtype):
    lane = lax.broadcasted_iota(jnp.int32, (1, PAIR), 1)
    low = (lane < HEAD).astype(F32)
    return low.astype(dtype), (1.0 - low).astype(dtype)


def causal_tile():
    shape = (TILE, TILE)
    return lax.broadcasted_iota(jnp.int32, shape, 0) <= lax.broadcasted_iota(jnp.int32, shape, 1)


def params(limit, *semantics):
    return pltpu.CompilerParams(
        vmem_limit_bytes=limit * MIB, dimension_semantics=semantics or ("arbitrary",)
    )


def cost(us):
    return pl.CostEstimate(flops=int(us * FLOPS), bytes_accessed=1000, transcendentals=0)


def call(kernel, name, us, grid, inputs, outputs, scratch, deps, place):
    any_ref = pl.BlockSpec(memory_space=pl.ANY)

    def body(place_ref, *refs):
        kernel(place_ref, *refs[len(deps) :])

    return pl.pallas_call(
        body,
        grid_spec=pltpu.PrefetchScalarGridSpec(
            num_scalar_prefetch=1,
            grid=grid,
            in_specs=[any_ref] * len(deps) + [pl.BlockSpec(b, i) for _, b, i in inputs],
            out_specs=[pl.BlockSpec(b, i) for _, _, b, i in outputs],
            scratch_shapes=scratch,
        ),
        out_shape=[jax.ShapeDtypeStruct(shape, kind) for shape, kind, _, _ in outputs],
        compiler_params=params(LIMIT, *["arbitrary"] * len(grid)),
        cost_estimate=cost(us),
        name=name,
    )(place, *deps, *[array for array, _, _ in inputs])


def whole(array):
    zeros = (0,) * array.ndim
    return array, array.shape, lambda *_: zeros


def same(*index):
    return lambda step, *_: index


def forward_kernel(
    place, tok, got, gain, wq, wk, wv, first, query, keys, values, core_own, core_far, stats, core
):
    half = got.shape[0]
    full = 2 * half
    here = pl.multiple_of(place[0] * half, half)
    there = pl.multiple_of((1 - place[0]) * half, half)

    @pl.when(pl.program_id(0) == 0)
    def _():
        first[pl.ds(here, half), :] = (normed(tok[0].astype(F32))[0] * gain[...]).astype(BF)
        first[pl.ds(there, half), :] = (normed(got[...].astype(F32))[0] * gain[...]).astype(BF)

    rows = first[...]
    query[...] = dot(rows, wq[...]).astype(BF)
    keys[...] = dot(rows, wk[...]).astype(BF)
    values[...] = dot(rows, wv[...]).astype(BF)
    masks = lane_masks(BF)
    values_t = values[...].T
    causal = causal_tile()
    tasks = [
        (head, block) for head in range(query.shape[1] // HEAD) for block in range(full // TILE)
    ]

    def score(head, block):
        pair = slice(head // 2 * PAIR, (head // 2 + 1) * PAIR)
        count = (block + 1) * TILE
        key_half = keys[:count, pair] * masks[head % 2]
        return dot_nt(key_half, query[block * TILE : count, pair])

    def soften(head, block, scores):
        count = (block + 1) * TILE
        near = jnp.where(causal, scores[count - TILE :], -1e30)
        if block > 0:
            near = jnp.concatenate([scores[: count - TILE], near], axis=0)
        top = jnp.max(near, axis=0, keepdims=True)
        powers = jnp.exp2((near - top) * SCALE2)
        total = jnp.sum(powers, axis=0, keepdims=True)
        stats[0, head : head + 1, block * TILE : count] = top * SCALE2 + jnp.log2(total)
        return powers.astype(BF), 1.0 / total

    def gather(head, block, powers, share):
        count = (block + 1) * TILE
        lanes = slice(head * HEAD, (head + 1) * HEAD)
        core[lanes, block * TILE : count] = dot(values_t[lanes, :count], powers) * share

    scores = score(*tasks[0])
    waiting = None
    for n, task in enumerate(tasks):
        ahead = score(*tasks[n + 1]) if n + 1 < len(tasks) else None
        softened = soften(*task, scores)
        if waiting is not None:
            gather(*waiting)
        waiting = task + softened
        scores = ahead
    gather(*waiting)
    core_own[...] = core[:, pl.ds(here, half)].T.astype(BF)
    core_far[...] = core[:, pl.ds(there, half)].T.astype(BF)


def attend(index, place, tokens, got, gain, wq, wk, wv):
    _, half, width = tokens.shape
    full = 2 * half
    quads = width // QUAD
    column = ((width, QUAD), lambda p, s: (0, p))
    wide = ((full, width), BF, (full, QUAD), lambda p, s: (0, p))
    part = ((half, width), BF, (half, QUAD), lambda p, s: (0, p))
    return call(
        forward_kernel,
        "attend_forward",
        13,
        (quads,),
        [
            (tokens, (1, half, width), lambda p, s: (2 * s[0] + index, 0, 0)),
            whole(got),
            whole(gain),
            (wq, *column),
            (wk, *column),
            (wv, *column),
        ],
        [
            ((full, width), BF, (full, width), same(0, 0)),
            wide,
            wide,
            wide,
            part,
            part,
            ((quads, 8, full), F32, (1, 8, full), lambda p, s: (p, 0, 0)),
        ],
        [pltpu.VMEM((QUAD, full), F32)],
        [],
        place,
    )


def mix_kernel(place, tok, cot, c0, c1, c2, c3, wo, gain, router, resid, merged, d_expert, gates):
    slots, rows, width = tok.shape
    attended = dot(jnp.concatenate([c0[...], c1[...], c2[...], c3[...]], axis=0), wo[...])
    seconds, logits, lives = [], [], []
    for r in range(slots):
        slot = lax.rem(r + 2 * place[0], slots)
        stream = tok[slot].astype(F32) + attended[r * rows : (r + 1) * rows]
        resid[r] = stream
        second = (normed(stream)[0] * gain[...]).astype(BF)
        seconds.append(second.astype(F32))
        live = slot < place[1]
        lives.append(live)
        logits.append(jnp.where(live, dot(second, router[...]), -1e30))
    top = jnp.maximum(jnp.maximum(logits[0], logits[1]), jnp.maximum(logits[2], logits[3]))
    powers = [jnp.where(lives[r], jnp.exp(logits[r] - top), 0.0) for r in range(slots)]
    total = powers[0] + powers[1] + powers[2] + powers[3]
    weights = []
    for r in range(slots):
        gate = powers[r] / total
        gates[r] = gate
        weights.append(gate.astype(BF).astype(F32))
    for e in range(2):
        both = jnp.zeros((rows, width), F32)
        back = jnp.zeros((rows, width), F32)
        for r in range(slots):
            slot = lax.rem(r + 2 * place[0], slots)
            weight = weights[r][:, e : e + 1]
            both = both + weight * seconds[r]
            back = back + weight * cot[slot].astype(F32)
        merged[e] = both.astype(BF)
        d_expert[e] = back.astype(BF)


def mix(place, tokens, cotangent, cores, output_weight, gain, router):
    slots, half, width = tokens.shape
    rows = 128
    quad = ((slots, rows, width), lambda p, s: (0, p, 0))
    part = ((rows, width), lambda p, s: (p, 0))
    twin = ((2, half, width), BF, (2, rows, width), lambda p, s: (0, p, 0))
    return call(
        mix_kernel,
        "mix",
        9,
        (half // rows,),
        [(tokens, *quad), (cotangent, *quad)]
        + [(core, *part) for core in cores]
        + [whole(output_weight), whole(gain), whole(router)],
        [
            ((slots, half, width), F32, *quad),
            twin,
            twin,
            ((slots, half, 128), F32, (slots, rows, 128), lambda p, s: (0, p, 0)),
        ],
        [],
        [],
        place,
    )


def expert_kernel(
    per, place, merged, d_expert, w_in, w_out, out, d_merged, keep, give, acc, d_acc, rows_t
):
    step = pl.program_id(0)
    rows = merged[0]
    back = d_expert[0]
    width = back.shape[1]
    root = math.sqrt(2.0 / math.pi)
    parts = w_in.shape[2] // TILE
    many = width // per
    mine = place[2] == 0

    @pl.when(step == 0)
    def _():
        rows_t[...] = rows.T

    def spans(n):
        return slice(n * TILE, (n + 1) * TILE)

    def ahead(n):
        return dot(rows, w_in[0, :, spans(n)]), dot_nt(back, w_out[0, spans(n), :])

    def bend(u, d_hidden):
        square = u * u
        bent = jnp.tanh(u * (root + (root * 0.044715) * square))
        hidden = (0.5 * u * (1.0 + bent)).astype(BF)
        slope = 0.5 * (1.0 + bent) + (0.5 * u) * (1.0 - bent * bent) * (
            root + (3.0 * root * 0.044715) * square
        )
        return hidden, (d_hidden * slope).astype(BF)

    def spread(n, hidden, d_pre):
        to_out = dot(hidden.T, back)
        to_out = jnp.concatenate([to_out[:, :TILE], to_out[:, TILE:]], axis=0)
        to_in = dot(rows_t[...], d_pre)
        shape = (many, per, TILE)
        at = slice(n * many, (n + 1) * many)
        keep[at] = jnp.where(mine, to_in, to_out).astype(BF).reshape(shape)
        give[at] = jnp.where(mine, to_out, to_in).astype(BF).reshape(shape)
        return dot(hidden, w_out[0, spans(n), :]), dot_nt(d_pre, w_in[0, :, spans(n)])

    forth, down, waiting = 0.0, 0.0, None
    current = ahead(0)
    for n in range(parts):
        later = ahead(n + 1) if n + 1 < parts else None
        bent = bend(*current)
        if waiting is not None:
            pair = spread(*waiting)
            forth, down = forth + pair[0], down + pair[1]
        waiting = (n,) + bent
        current = later
    pair = spread(*waiting)
    forth, down = forth + pair[0], down + pair[1]

    @pl.when(step == 0)
    def _():
        acc[...] = forth
        d_acc[...] = down

    @pl.when(step == pl.num_programs(0) - 1)
    def _():
        out[...] = (acc[...] + forth).astype(BF)
        d_merged[...] = (d_acc[...] + down).astype(BF)


def expert(e, place, count, merged, d_expert, w_in, w_out, deps):
    _, rows, width = merged.shape
    hidden = w_in.shape[2]
    chunk = hidden // 2
    per = hidden // TILE * width // count
    one = ((1, rows, width), same(e, 0, 0))
    flat = ((rows, width), BF, (rows, width), same(0, 0))
    part = ((count, per, TILE), BF, (count // 2, per, TILE), lambda f, s: (f, 0, 0))
    return call(
        lambda *refs: expert_kernel(per, *refs),
        "expert",
        13,
        (2,),
        [
            (merged, *one),
            (d_expert, *one),
            (w_in, (1, width, chunk), lambda f, s: (e, 0, f)),
            (w_out, (1, chunk, width), lambda f, s: (e, f, 0)),
        ],
        [flat, flat, part, part],
        [
            pltpu.VMEM((rows, width), F32),
            pltpu.VMEM((rows, width), F32),
            pltpu.VMEM((width, rows), BF),
        ],
        deps,
        place,
    )


def low_kernel(
    place, resid, cot, gates, x0, x1, m0, m1, router, gain, d2, d3, d0, lows_out, g_router, g_gain
):
    slots, rows, width = resid.shape
    outs = [x0[...].astype(F32), x1[...].astype(F32)]
    downs = [m0[...].astype(F32), m1[...].astype(F32)]
    lane = lax.broadcasted_iota(jnp.int32, (rows, 128), 1)
    hats, inverses, seconds, d_gates = [], [], [], []
    for r in range(slots):
        slot = lax.rem(r + 2 * place[0], slots)
        hat, inverse = normed(resid[r])
        second = (hat * gain[...]).astype(BF)
        hats.append(hat)
        inverses.append(inverse)
        seconds.append(second)
        cotangent = cot[slot].astype(F32)
        second = second.astype(F32)
        columns = [
            jnp.sum(cotangent * outs[e] + downs[e] * second, axis=-1, keepdims=True)
            for e in range(2)
        ]
        d_gates.append(jnp.where(lane == 0, columns[0], jnp.where(lane == 1, columns[1], 0.0)))
    mean = sum(gates[r] * d_gates[r] for r in range(slots))
    lows = [(gates[r] * (d_gates[r] - mean)).astype(BF) for r in range(slots)]
    gain_sum = jnp.zeros((1, width), F32)
    for r in range(slots):
        low = lows[r].astype(F32)
        lows_out[r] = low
        if r != 1:
            d_rows, gain_part = resid_back(
                cot[lax.rem(r + 2 * place[0], slots)], gates[r], low, downs, router, gain,
                hats[r], inverses[r],
            )
            {2: d2, 3: d3, 0: d0}[r][...] = d_rows
            gain_sum = gain_sum + gain_part
    low_rows = jnp.concatenate(lows, axis=0).astype(F32).T[:8].astype(BF)
    router_sum = dot(low_rows, jnp.concatenate(seconds, axis=0))
    add_up(g_router, router_sum)
    add_up(g_gain, jnp.broadcast_to(gain_sum, (8, width)))


def add_up(ref, value):
    @pl.when(pl.program_id(0) == 0)
    def _():
        ref[...] = value

    @pl.when(pl.program_id(0) > 0)
    def _():
        ref[...] += value


def resid_back(cotangent, gate, low, downs, router, gain, hat, inverse):
    weight = gate.astype(BF).astype(F32)
    d_second = sum(
        weight[:, e : e + 1] * downs[e] + low[:, e : e + 1] * router[e : e + 1, :]
        for e in range(2)
    )
    d_stream = norm_back(d_second * gain[...], hat, inverse)
    d_rows = (cotangent.astype(F32) + d_stream).astype(BF)
    return d_rows, jnp.sum(d_second * hat, axis=0, keepdims=True)


def own_kernel(
    place, resid, cot, gates, lows, m0, m1, router, gain, c0, c1, c2, c3, d0, d2, d3, g_router,
    g_gain_far, d1, keep, give, g_gain, g_out,
):
    step = pl.program_id(0)
    width = resid.shape[2]
    downs = [m0[...].astype(F32), m1[...].astype(F32)]
    hat, inverse = normed(resid[0])
    d_rows, gain_part = resid_back(
        cot[0], gates[0], lows[0], downs, router, gain, hat, inverse
    )
    d1[...] = d_rows
    add_up(g_gain, jnp.broadcast_to(gain_part, (8, width)))
    cores = jnp.concatenate([c0[...], c1[...], c2[...], c3[...]], axis=0)
    rows = jnp.concatenate([d0[...], d_rows, d2[...], d3[...]], axis=0)
    total = dot(cores.T, rows)

    add_up(g_out, total)

    @pl.when(step == pl.num_programs(0) - 1)
    def _():
        mine = place[2] == 0
        low, high = g_out[:, :TILE], g_out[:, TILE:]
        line = lax.broadcasted_iota(jnp.int32, (8, width), 0)
        small = jnp.where(line < 2, g_router[...], 0.0)
        small = jnp.where(line == 2, g_gain_far[...] + g_gain[...], small)
        small = jnp.concatenate(
            [small[:, :TILE], small[:, TILE:], jnp.zeros((width - 16, TILE), F32)], axis=0
        )
        blank = jnp.zeros((width, TILE), F32)
        one = jnp.concatenate([jnp.where(mine, low, high), jnp.where(mine, small, blank)])
        two = jnp.concatenate([jnp.where(mine, high, low), jnp.where(mine, blank, small)])
        keep[...] = one.astype(BF)
        give[...] = two.astype(BF)


def output_kernel(place, resid, gates, x0, x1, output):
    slots = resid.shape[0]
    outs = [x0[...].astype(F32), x1[...].astype(F32)]
    for r in range(slots):
        slot = lax.rem(r + 2 * place[0], slots)
        weight = gates[r].astype(BF).astype(F32)
        output[slot] = (
            resid[r] + weight[:, 0:1] * outs[0] + weight[:, 1:2] * outs[1]
        ).astype(BF)


def blocks_of(slots, rows, width):
    return dict(
        quad=((slots, rows, width), lambda p, s: (0, p, 0)),
        other=((1, rows, width), lambda p, s: (1, p, 0)),
        our_other=((1, rows, width), lambda p, s: (2 * s[0] + 1, p, 0)),
        other_lanes=((1, rows, 128), lambda p, s: (1, p, 0)),
        lanes=((slots, rows, 128), lambda p, s: (0, p, 0)),
        part=((rows, width), lambda p, s: (p, 0)),
        eight=((8, width), same(0, 0)),
    )


def unmix_far(place, resid, cotangent, gates, outs, downs, router, gain, deps):
    slots, half, width = resid.shape
    b = blocks_of(slots, 128, width)
    return call(
        low_kernel,
        "unmix_far",
        9,
        (half // 128,),
        [(resid, *b["quad"]), (cotangent, *b["quad"]), (gates, *b["lanes"])]
        + [(value, *b["part"]) for value in (*outs, *downs)]
        + [whole(router), whole(gain)],
        [((half, width), BF, *b["part"])] * 3
        + [((slots, half, 128), F32, *b["lanes"])]
        + [((8, width), F32, *b["eight"])] * 2,
        [],
        deps,
        place,
    )


def unmix_own(
    place, resid, cotangent, gates, lows, downs, router, gain, cores, d_rows, g_router, gain_far, deps
):
    slots, half, width = resid.shape
    b = blocks_of(slots, 128, width)
    rest = ((2 * width, TILE), BF, (2 * width, TILE), same(0, 0))
    return call(
        own_kernel,
        "unmix_own",
        1,
        (half // 128,),
        [(resid, *b["other"]), (cotangent, *b["our_other"])]
        + [(value, *b["other_lanes"]) for value in (gates, lows)]
        + [(value, *b["part"]) for value in downs]
        + [whole(router), whole(gain)]
        + [(value, *b["part"]) for value in (*cores, *d_rows)]
        + [whole(g_router), whole(gain_far)],
        [((half, width), BF, *b["part"]), rest, rest],
        [pltpu.VMEM((8, width), F32), pltpu.VMEM((width, width), F32)],
        deps,
        place,
    )


def write_output(place, resid, gates, outs, deps):
    slots, half, width = resid.shape
    b = blocks_of(slots, 128, width)
    return call(
        output_kernel,
        "write_output",
        1,
        (half // 128,),
        [(resid, *b["quad"]), (gates, *b["lanes"])] + [(value, *b["part"]) for value in outs],
        [((slots, half, width), BF, *b["quad"])],
        [],
        deps,
        place,
    )[0]


def backward_kernel(
    place, d_own, d_got, query, keys, values, core_own, core_far, stats, wo, three,
    d_attn, core, dq_t, d_keys, d_values,
):
    half = d_own.shape[0]
    full = 2 * half
    here = pl.multiple_of(place[0] * half, half)
    there = pl.multiple_of((1 - place[0]) * half, half)
    d_attn[pl.ds(here, half), :] = d_own[...]
    d_attn[pl.ds(there, half), :] = d_got[...]
    core[pl.ds(here, half), :] = core_own[...]
    core[pl.ds(there, half), :] = core_far[...]
    d_core = dot_nt(d_attn[...], wo[...]).astype(BF)
    product = (d_core.astype(F32) * core[...].astype(F32)).T
    masks = lane_masks(BF)
    keys_t = keys[...].T
    causal = causal_tile()
    tasks = [
        (head, block) for head in range(query.shape[1] // HEAD) for block in range(full // TILE)
    ]

    def of_pair(head):
        return slice(head // 2 * PAIR, (head // 2 + 1) * PAIR)

    def score(head, block):
        pair, mask, count = of_pair(head), masks[head % 2], (block + 1) * TILE
        span = slice(block * TILE, count)
        scores = dot_nt(keys[:count, pair] * mask, query[span, pair])
        d_probs = dot_nt(values[:count, pair] * mask, d_core[span, pair])
        return scores, d_probs

    def soften(head, block, scores, d_probs):
        count = (block + 1) * TILE
        span = slice(block * TILE, count)
        delta = jnp.sum(product[head * HEAD : (head + 1) * HEAD, span], axis=0, keepdims=True)
        probs = jnp.exp2(scores * SCALE2 - stats[0, head : head + 1, span])
        near = jnp.where(causal, probs[count - TILE :], 0.0)
        if block > 0:
            near = jnp.concatenate([probs[: count - TILE], near], axis=0)
        return near.astype(BF), (near * (d_probs - delta)).astype(BF)

    def spread(head, block, probs, d_scores):
        pair, mask, count = of_pair(head), masks[head % 2], (block + 1) * TILE
        span, before = slice(block * TILE, count), slice(0, count - TILE)
        lanes = slice(head * HEAD, (head + 1) * HEAD)
        to_value = dot(probs, d_core[span, pair] * mask)
        to_key = dot(d_scores, query[span, pair] * mask)
        if head % 2 == 0:
            d_values[span, pair] = to_value[count - TILE :]
            d_keys[span, pair] = to_key[count - TILE :]
            if block > 0:
                d_values[before, pair] += to_value[before]
                d_keys[before, pair] += to_key[before]
        else:
            d_values[:count, pair] += to_value
            d_keys[:count, pair] += to_key
        dq_t[lanes, span] = dot(keys_t[lanes, :count], d_scores)

    scored = score(*tasks[0])
    waiting = None
    for n, task in enumerate(tasks):
        ahead = score(*tasks[n + 1]) if n + 1 < len(tasks) else None
        softened = soften(*task, *scored)
        if waiting is not None:
            spread(*waiting)
        waiting = task + softened
        scored = ahead
    spread(*waiting)
    three[:, :QUAD] = (dq_t[...].T * SCALE).astype(BF)
    three[:, QUAD : 2 * QUAD] = (d_keys[...] * SCALE).astype(BF)
    three[:, 2 * QUAD :] = d_values[...].astype(BF)


def attend_back(us, quads, place, d_own, d_got, kept, wo, deps):
    first, query, keys, values, core_own, core_far, stats = kept
    half, width = d_own.shape
    full = 2 * half
    start, count = quads

    def column(rows):
        return (rows, QUAD), lambda p, s: (0, start + p)

    return call(
        backward_kernel,
        "attend_backward",
        us,
        (count,),
        [
            whole(d_own),
            whole(d_got),
            (query, *column(full)),
            (keys, *column(full)),
            (values, *column(full)),
            (core_own, *column(half)),
            (core_far, *column(half)),
            (stats, (1, 8, full), lambda p, s: (start + p, 0, 0)),
            (wo, (QUAD, width), lambda p, s: (start + p, 0)),
        ],
        [((full, count * 3 * QUAD), BF, (full, 3 * QUAD), lambda p, s: (0, p))],
        [
            pltpu.VMEM((full, width), BF),
            pltpu.VMEM((full, QUAD), BF),
            pltpu.VMEM((QUAD, full), F32),
            pltpu.VMEM((full, QUAD), F32),
            pltpu.VMEM((full, QUAD), F32),
        ],
        deps,
        place,
    )[0]


def first_kernel(place, t0, t1, own, got, gain, wq, wk, wv, d_tok_own, d_tok_far):
    d_first = 0.0
    for quad, three in enumerate((t0, t1)):
        lanes = slice(quad * QUAD, (quad + 1) * QUAD)
        weights = [w[:, lanes] for w in (wq, wk, wv)]
        d_first = d_first + dot_nt(three[...], jnp.concatenate(weights, axis=1))
    near = pl.program_id(0) == 0
    value = jnp.where(near, own[0].astype(F32), got[...].astype(F32))
    hat, inverse = normed(value)
    result = norm_back(d_first * gain[...], hat, inverse).astype(BF)

    @pl.when(near)
    def _():
        d_tok_own[...] = result

    @pl.when(jnp.logical_not(near))
    def _():
        d_tok_far[...] = result


def first_back(us, index, place, threes, tokens, got, gain, weights, deps):
    _, half, width = tokens.shape
    rows = 256
    blocks = half // rows

    def row_block(h, j, s):
        return jnp.where(h == 0, s[0], 1 - s[0]) * blocks + j

    return call(
        first_kernel,
        "first_back",
        us,
        (2, blocks),
        [
            (three, (rows, 3 * QUAD), lambda h, j, s, c=c: (row_block(h, j, s), c))
            for three, c in threes
        ]
        + [
            (
                tokens,
                (1, rows, width),
                lambda h, j, s: (2 * s[0] + index, jnp.where(h == 0, j, blocks - 1), 0),
            ),
            (got, (rows, width), lambda h, j, s: (jnp.where(h == 0, 0, j), 0)),
            whole(gain),
            *[whole(weight) for weight in weights],
        ],
        [
            (
                (half, width),
                BF,
                (rows, width),
                lambda h, j, s: (jnp.where(h == 0, j, blocks - 1), 0),
            ),
            ((half, width), BF, (rows, width), lambda h, j, s: (jnp.where(h == 0, 0, j), 0)),
        ],
        [],
        deps,
        place,
    )


def project_kernel(place, f0, f1, a0, a1, b0, b1, keep, give, t0, t1):
    @pl.when(pl.program_id(0) == 0)
    def _():
        t0[...] = f0[...].T
        t1[...] = f1[...].T

    mine = place[2] == 0
    low = dot(t0[...], a0[...]) + dot(t1[...], b0[...])
    high = dot(t0[...], a1[...]) + dot(t1[...], b1[...])
    keep[...] = jnp.where(mine, low, high).astype(BF)
    give[...] = jnp.where(mine, high, low).astype(BF)


def project_grads(place, firsts, threes, deps):
    full, width = firsts[0].shape
    out = ((3 * width, QUAD), BF, (width, QUAD), lambda p, s: (p, 0))
    return call(
        project_kernel,
        "project_grads",
        1,
        (3,),
        [whole(first) for first in firsts]
        + [
            (three, (full, QUAD), lambda p, s, c=c: (0, 3 * c + p))
            for pair in threes
            for three, c in pair
        ],
        [out, out],
        [pltpu.VMEM((width, full), BF), pltpu.VMEM((width, full), BF)],
        deps,
        place,
    )


def chip_bits(devices):
    return [1] + [1 << n for n in range(2, devices.bit_length() - 1)]


def masks_of(level):
    return [level[0], level[1], level[0] + level[1]] if len(level) > 1 else [level[0]]


def send(value, mask, devices):
    return lax.ppermute(value, AXES, [(n, n ^ mask) for n in range(devices)])


class Summed:
    def __init__(self, lanes, devices, levels, lane_levels):
        self.devices, self.levels, self.lane_levels = devices, levels, lane_levels
        self.steps, self.count, self.parts = 0, len(levels), None
        self.arrays, self.orders, self.rows = [], [], []
        for lane, own in zip(lanes, lane_levels):
            self.arrays += [[keep, send(give, 2, devices)] for keep, give in lane]
            order = own[0] if len(own) == 1 else [bit for level in reversed(own) for bit in level]
            self.orders += [order] * len(lane)
            self.rows.append(sum(keep.shape[1] for keep, _ in lane))

    def jobs(self):
        n = self.steps
        if n == 0:
            return [(self.arrays, self.levels[0], self.orders)]
        if n <= self.count:
            level = self.levels[n] if n < self.count else []
            return [(self.arrays, level, [level] * len(self.arrays))]
        if self.parts is not None:
            return [(part, None, [part[0][0].shape[1]]) for part in self.parts]
        return [(self.arrays, None, self.rows if n == 2 * self.count - 1 else [sum(self.rows)])]

    def take(self, results):
        n, count = self.steps, self.count
        self.steps += 1
        if n < count:
            mine, *others = results[0]
            masks = masks_of(self.levels[n])
            got = [send(other, mask, self.devices) for other, mask in zip(others, masks)]
            self.arrays = [[mine] + got]
            return
        values = [value for result in results for value in result]
        if n < 2 * count - 1:
            masks = masks_of(self.levels[2 * count - 1 - n])
            self.arrays = [values + [send(values[0], mask, self.devices) for mask in masks]]
            return
        self.parts = []
        for own, value in zip(self.lane_levels, values):
            masks = masks_of(own[len(own) - 1 - (n - 2 * count + 1)])
            self.parts.append([[value] + [send(value, mask, self.devices) for mask in masks]])

    def done(self):
        return self.steps >= 2 * self.count - 1 + len(self.lane_levels[0])

    def exchange(self):
        self.early = [send(part[0][0], 2, self.devices) for part in self.parts]
        return self.early

    def finish(self):
        return [
            part[0] + [first] + [send(some, 2, self.devices) for some in part[0][1:]]
            for part, first in zip(self.parts, self.early)
        ]


def step_kernel(kinds, place, *refs):
    ins = sum(sum(groups) for _, groups, _ in kinds)
    inputs, outputs = refs[:ins], refs[ins:]
    for adds, groups, n_out in kinds:
        here, inputs = inputs[: sum(groups)], inputs[sum(groups) :]
        there, outputs = outputs[:n_out], outputs[n_out:]
        if not adds:
            size, row = here[0].shape[0], 0
            for target in there:
                rows = target.shape[1]
                for n, ref in enumerate(here):
                    target[n * size : (n + 1) * size] = ref[:, row : row + rows, :]
                row += rows
            continue
        for target in there:
            row = 0
            for each in groups[: len(groups) // n_out]:
                total = here[0][...].astype(F32)
                for other in here[1:each]:
                    total = total + other[...].astype(F32)
                here, rows = here[each:], total.shape[1]
                target[:, row : row + rows, :] = total.astype(BF)
                row += rows


def advance(chains, place, deps, us=3):
    jobs = [chain.jobs() for chain in chains]
    every = [job for some in jobs for job in some]
    splits = [arrays[0][0].shape[0] >> len(level or []) for arrays, level, _ in every]
    big = max(array[0].size for arrays, _, _ in every for array in arrays)
    steps = max(1, 2 * big // MIB) if all(level is not None for _, level, _ in every) else 1
    steps = min([steps] + splits)
    inputs, outputs, kinds = [], [], []
    for (arrays, level, orders), split in zip(every, splits):
        width = arrays[0][0].shape[2]
        if level is None:
            count = split * len(arrays[0])
            inputs += [whole(array) for array in arrays[0]]
            for rows in orders:
                shape = (count, rows, width)
                outputs.append((shape, BF, shape, lambda p, s: (0, 0, 0)))
            kinds.append((False, [len(arrays[0])], len(orders)))
            continue
        block = split // steps
        rows = sum(some[0].shape[1] for some in arrays)

        def index(mask, order):
            def at(p, s):
                own = 0
                for n, bit in enumerate(order):
                    own = own + (lax.rem(s[4] // bit + (1 if mask & bit else 0), 2) << n)
                return (own * steps + p, 0, 0)

            return at

        for mask in [0] + (masks_of(level) if level else []):
            for some, order in zip(arrays, orders):
                inputs += [(a, (block,) + a.shape[1:], index(mask, order)) for a in some]
            outputs.append(
                ((split, rows, width), BF, (block, rows, width), lambda p, s: (p, 0, 0))
            )
        n_out = 1 << len(level)
        kinds.append((True, [len(some) for some in arrays] * n_out, n_out))
    results = call(
        lambda *refs: step_kernel(kinds, *refs), "sum_step", us, (steps,), inputs, outputs, [],
        deps, place,
    )
    mark, groups = results[0], []
    for _, _, n_out in kinds:
        groups.append(results[:n_out])
        results = results[n_out:]
    for chain, some in zip(chains, jobs):
        chain.take(groups[: len(some)])
        groups = groups[len(some) :]
    return [mark]


def result_kernel(per, each, experts, place, *refs):
    held, (grad_in, grad_out) = refs[:-2], refs[-2:]
    mine = place[2] == 0
    half = each // 2
    for n, e in enumerate(experts):

        @pl.when(pl.program_id(0) == n)
        def _():
            own, other = held[2 * n : 2 * n + 2]
            swap = place[3 + 2 * e] & (each - 1)
            for t in range(each):
                first, second = own[t ^ swap].astype(F32), other[t ^ swap].astype(F32)
                low, high = jnp.where(mine, first, second), jnp.where(mine, second, first)
                grad_in[0, t * per : (t + 1) * per, :] = low
                lanes = slice(t // half * TILE, (t // half + 1) * TILE)
                grad_out[0, t % half * per : (t % half + 1) * per, lanes] = high


def expert_results(experts, d, place, parts, width, hidden, per, earlier, deps):
    inner = parts[0][0].shape[0]
    each = width // per
    blocks = inner // each

    def chip(e, s):
        return s[3 + 2 * e]

    def expert(n):
        return n + experts[0]

    def piece(n, k, s):
        some = jnp.where(expert(n) == 0, s[3], s[5])
        return (d ^ (some // inner)) * blocks + k

    def part_index(own):
        def index(n, k, s):
            e, first = expert(n), (chip(own, s) % inner) // each
            at = jnp.where(e == own, k, jnp.where(e < own, 0, blocks - 1))
            return (at ^ first, 0, 0)

        return index

    inputs = []
    for e in experts:
        inputs += [
            (parts[e][n], (each, per, TILE), part_index(e)) for n in (d, len(parts[e]) // 2 + d)
        ]
    outputs = [
        ((2, width, hidden), F32, (1, width, TILE), lambda n, k, s: (expert(n), 0, piece(n, k, s))),
        ((2, hidden, width), F32, (1, TILE, width), lambda n, k, s: (expert(n), piece(n, k, s), 0)),
    ]
    any_ref = pl.BlockSpec(memory_space=pl.ANY)
    held = len(earlier) + len(deps)

    def body(place_ref, *refs):
        result_kernel(per, each, experts, place_ref, *refs[held:])

    return pl.pallas_call(
        body,
        grid_spec=pltpu.PrefetchScalarGridSpec(
            num_scalar_prefetch=1,
            grid=(len(experts), blocks),
            in_specs=[any_ref] * held + [pl.BlockSpec(b, i) for _, b, i in inputs],
            out_specs=[pl.BlockSpec(b, i) for _, _, b, i in outputs],
        ),
        out_shape=[jax.ShapeDtypeStruct(shape, kind) for shape, kind, _, _ in outputs],
        input_output_aliases={1 + n: n for n in range(len(earlier))},
        compiler_params=params(LIMIT, "arbitrary", "arbitrary"),
        cost_estimate=cost(5 * len(experts)),
        name="expert_results",
    )(place, *earlier, *deps, *[array for array, _, _ in inputs])


def project_result_kernel(place, *refs):
    count = (len(refs) - 13) // 2
    parts, others = refs[:count], refs[count : 2 * count]
    weights, gain = refs[2 * count : 2 * count + 3], refs[2 * count + 3]
    grads = refs[2 * count + 4 : 2 * count + 8]
    g_gain, g_gain2, g_router, halves, rest = refs[2 * count + 8 :]
    inner, rows, _ = parts[0].shape
    width = gain.shape[1]
    per = 3 * width // (count * inner)
    for d in range(count):
        for m in range(inner):
            shard = (d * inner + m) ^ place[3]
            at = pl.ds(pl.multiple_of(shard * per, 8), per)
            more = pl.ds(pl.multiple_of(shard * (rows - per), 8), rows - per)
            for half, source in ((place[2], parts), (1 - place[2], others)):
                value = source[d][m].astype(F32)
                halves[half, at, :] = value[:per]
                rest[half, more, :] = value[per:]
    total = jnp.zeros((width, 1), F32)
    for n in range(4):
        for h in range(2):
            lanes = slice(h * QUAD, (h + 1) * QUAD)
            if n == 3:
                grads[n][:, lanes] = rest[h, :width, :]
                continue
            value = halves[h, n * width : (n + 1) * width, :]
            grads[n][:, lanes] = value
            total += jnp.sum(value * weights[n][:, lanes].astype(F32), axis=1, keepdims=True)
    g_gain[...] = jnp.broadcast_to(total, (width, 128)).T[:1] / gain[...]
    for h in range(2):
        lanes = slice(h * QUAD, (h + 1) * QUAD)
        small = rest[0, width + 8 * h : width + 8 * (h + 1), :]
        g_router[:, lanes] = small[:2]
        g_gain2[:, lanes] = small[2:3]


def project_result(place, chip, parts, weights, gain, deps):
    width = gain.shape[1]
    square = ((width, width), F32, (width, width), same(0, 0))
    line = ((1, width), F32, (1, width), same(0, 0))
    return call(
        project_result_kernel,
        "project_result",
        1,
        (1,),
        [whole(value) for value in (*parts, *weights, gain)],
        [square] * 4 + [line, line, ((2, width), F32, (2, width), same(0, 0))],
        [pltpu.VMEM((2, 3 * width, QUAD), F32), pltpu.VMEM((2, 2 * width, QUAD), F32)],
        deps,
        place.at[3].set(chip),
    )


def shards(
    tokens, seq_counts, norm1_gain, w_query, w_key, w_value, output_weight, norm2_gain,
    router_weight, w_expert_in, w_expert_out, cotangent,
):
    slots, half, width = tokens.shape
    hidden = w_expert_in.shape[2]
    devices = lax.axis_size("dp") * lax.axis_size("blk")
    count = devices // 2
    blk = lax.axis_index("blk")
    dp = lax.axis_index("dp")
    me = dp * 2 + blk
    core_bit = lax.rem(dp, 2)
    bits = chip_bits(devices)
    x, y, *more = bits
    levels = [bits[n : n + 2] for n in range(0, len(bits), 2)]
    lanes = [[[y], [x]], [[x], [y]]]

    def chip_of(levels):
        chip = jnp.int32(0)
        for level in levels:
            for bit in reversed(level):
                chip = chip * 2 + lax.rem(me // bit, 2)
        return chip

    place = jnp.stack([blk, seq_counts[0], core_bit, jnp.int32(0), me]).astype(jnp.int32)
    gain1 = norm1_gain.reshape(1, width)
    gain2 = norm2_gain.reshape(1, width)
    router = jnp.pad(router_weight, ((0, 0), (0, 126)))
    router_rows = jnp.pad(router_weight.T.astype(F32), ((0, 6), (0, 0)))
    weights = (w_query, w_key, w_value)

    def swap(value):
        return send(value, 1, devices)

    far = [
        lax.dynamic_index_in_dim(tokens, lax.rem(2 + i + 2 * blk, 4), 0, keepdims=False)
        for i in range(2)
    ]
    got = [swap(value) for value in far]
    kept = [
        attend(i, place, tokens, got[i], gain1, w_query, w_key, w_value) for i in range(2)
    ]
    cores = [kept[0][4], kept[1][4], swap(kept[0][5]), swap(kept[1][5])]
    resid, merged, d_expert, gates = mix(
        place, tokens, cotangent, cores, output_weight, gain2, router
    )
    per = hidden // TILE * width // count
    done = [expert(0, place, count, merged, d_expert, w_expert_in, w_expert_out, [])]
    done.append(
        expert(1, place, count, merged, d_expert, w_expert_in, w_expert_out, [done[0][0]])
    )
    outs, downs = [d[0] for d in done], [d[1] for d in done]
    summed = Summed([[done[0][2:4]], [done[1][2:4]]], devices, levels, lanes)
    d2, d3, d0, lows, g_router, gain_far = unmix_far(
        place, resid, cotangent, gates, outs, downs, router_rows, gain2, []
    )
    d_got = [swap(d2), swap(d3)]
    marks = advance([summed], place, [d2])

    a = attend_back(30, (0, 2), place, d0, d_got[0], kept[0], output_weight, marks)
    d1, *rest = unmix_own(
        place, resid, cotangent, gates, lows, downs, router_rows, gain2, cores, [d0, d2, d3],
        g_router, gain_far, [a],
    )
    rest = [value.reshape(count, -1, TILE) for value in rest]
    threes = [[(a, 0), (a, 1)]]
    far_a = first_back(1, 0, place, threes[0], tokens, got[0], gain1, weights, [d1, d_got[1]])
    t_far = [swap(far_a[1])]

    def back(quad, us, deps):
        return attend_back(us, (quad, 1), place, d1, d_got[1], kept[1], output_weight, deps)

    b0 = back(0, 1, [far_a[0]])
    b1 = back(1, 20, [t_far[0]] + advance([summed], place, [b0]))
    threes.append([(b0, 0), (b1, 0)])
    pair = project_grads(place, [kept[0][0], kept[1][0]], threes, [b1])
    pair = [value.reshape(count, -1, QUAD) for value in pair]
    last = Summed([[pair, rest]], devices, levels, [levels[:1]])
    marks = advance([summed], place, [pair[0]])
    marks = advance([last], place, marks)
    far_b = first_back(6, 1, place, threes[1], tokens, got[1], gain1, weights, marks)
    t_far.append(swap(far_b[1]))
    marks = advance([summed, last], place, [far_b[0]])
    output = write_output(place, resid, gates, outs, marks)
    marks = advance([last], place, [output], 1)
    while not summed.done():
        marks = advance([summed], place, marks + [t_far[1]], 1)
    marks = marks + summed.exchange()
    while not last.done():
        marks = advance([last], place, marks, 1)
    last.exchange()
    own = [
        (d.astype(F32) + t.astype(F32)).astype(BF)
        for d, t in zip((d0, d1), (far_a[0], far_b[0]))
    ]
    other = [(d.astype(F32) + t.astype(F32)).astype(BF) for d, t in zip((d2, d3), t_far)]
    grad_tokens = jnp.where(blk == 0, jnp.stack(own + other), jnp.stack(other + own))
    parts = summed.finish()
    chips = [chip_of(lane + levels[1:]) for lane in lanes]
    final = jnp.stack([blk, seq_counts[0], core_bit, chips[0], me, chips[1]]).astype(jnp.int32)
    results = []
    for e in range(2):
        results = expert_results((e,), 0, final, parts, width, hidden, per, results, [])
    grad_in, grad_out = expert_results(
        (0, 1), 1, final, parts, width, hidden, per, results, []
    )
    *grads, grad_gain1, grad_gain2, grad_router = project_result(
        place, chip_of(levels), last.finish()[0], weights, gain1, [grad_in]
    )
    return (
        output, grad_tokens, grad_gain1.reshape(width), *grads, grad_gain2.reshape(width),
        grad_router.T, grad_in, grad_out,
    )


def solution(mesh):
    data = P("dp", "blk", None)
    return jax.shard_map(
        shards,
        mesh=mesh,
        in_specs=(data, P("dp")) + (P(),) * 9 + (data,),
        out_specs=(data, data) + (P(),) * 9,
        check_vma=False,
    )
```

```python
import math

import jax
import jax.numpy as jnp
from jax import lax
from jax.experimental import pallas as pl
from jax.experimental.pallas import tpu as pltpu
from jax.sharding import PartitionSpec as P

HEADS = 8
HEAD = 64
PAIR = 2 * HEAD
QUAD = 4 * HEAD
EPS = 1e-05
SCALE = HEAD ** (-0.5)
SCALE2 = SCALE * math.log2(math.e)
TILE = 256
BF = jnp.bfloat16
F32 = jnp.float32
AXES = ("dp", "blk")
MIB = 1 << 20
LIMIT = 64
FLOPS = 2_000_000_000


def dot(left, right):
    return jnp.dot(left, right, preferred_element_type=F32)


def dot_nt(left, right):
    return lax.dot_general(left, right, (((1,), (1,)), ((), ())), preferred_element_type=F32)


def dot_tn(left, right):
    return lax.dot_general(left, right, (((0,), (0,)), ((), ())), preferred_element_type=F32)


def normed(value):
    center = value - jnp.mean(value, axis=-1, keepdims=True)
    inverse = lax.rsqrt(jnp.mean(center * center, axis=-1, keepdims=True) + EPS)
    return center * inverse, inverse


def norm_back(scaled, hat, inverse):
    return inverse * (
        scaled
        - jnp.mean(scaled, axis=-1, keepdims=True)
        - hat * jnp.mean(scaled * hat, axis=-1, keepdims=True)
    )


def lane_masks(dtype):
    lane = lax.broadcasted_iota(jnp.int32, (1, PAIR), 1)
    low = (lane < HEAD).astype(F32)
    return low.astype(dtype), (1.0 - low).astype(dtype)


def causal_tile():
    shape = (TILE, TILE)
    return lax.broadcasted_iota(jnp.int32, shape, 0) <= lax.broadcasted_iota(jnp.int32, shape, 1)


def params(limit, *semantics):
    return pltpu.CompilerParams(
        vmem_limit_bytes=limit * MIB, dimension_semantics=semantics or ("arbitrary",)
    )


def cost(us):
    return pl.CostEstimate(flops=int(us * FLOPS), bytes_accessed=1000, transcendentals=0)


def call(kernel, name, us, grid, inputs, outputs, scratch, deps, place):
    any_ref = pl.BlockSpec(memory_space=pl.ANY)

    def body(place_ref, *refs):
        kernel(place_ref, *refs[len(deps) :])

    return pl.pallas_call(
        body,
        grid_spec=pltpu.PrefetchScalarGridSpec(
            num_scalar_prefetch=1,
            grid=grid,
            in_specs=[any_ref] * len(deps) + [pl.BlockSpec(b, i) for _, b, i in inputs],
            out_specs=[pl.BlockSpec(b, i) for _, _, b, i in outputs],
            scratch_shapes=scratch,
        ),
        out_shape=[jax.ShapeDtypeStruct(shape, kind) for shape, kind, _, _ in outputs],
        compiler_params=params(LIMIT, *["arbitrary"] * len(grid)),
        cost_estimate=cost(us),
        name=name,
    )(place, *deps, *[array for array, _, _ in inputs])


def whole(array):
    zeros = (0,) * array.ndim
    return array, array.shape, lambda *_: zeros


def same(*index):
    return lambda step, *_: index


def forward_kernel(
    place, tok, got, gain, wq, wk, wv, first, query, keys, values, core_own, core_far, stats, core
):
    half = got.shape[0]
    full = 2 * half
    here = pl.multiple_of(place[0] * half, half)
    there = pl.multiple_of((1 - place[0]) * half, half)

    @pl.when(pl.program_id(0) == 0)
    def _():
        first[pl.ds(here, half), :] = (normed(tok[0].astype(F32))[0] * gain[...]).astype(BF)
        first[pl.ds(there, half), :] = (normed(got[...].astype(F32))[0] * gain[...]).astype(BF)

    rows = first[...]
    query[...] = dot(rows, wq[...]).astype(BF)
    keys[...] = dot(rows, wk[...]).astype(BF)
    values[...] = dot(rows, wv[...]).astype(BF)
    masks = lane_masks(BF)
    values_t = values[...].T
    causal = causal_tile()
    tasks = [
        (head, block) for head in range(query.shape[1] // HEAD) for block in range(full // TILE)
    ]

    def score(head, block):
        pair = slice(head // 2 * PAIR, (head // 2 + 1) * PAIR)
        count = (block + 1) * TILE
        key_half = keys[:count, pair] * masks[head % 2]
        return dot_nt(key_half, query[block * TILE : count, pair])

    def soften(head, block, scores):
        count = (block + 1) * TILE
        near = jnp.where(causal, scores[count - TILE :], -1e30)
        if block > 0:
            near = jnp.concatenate([scores[: count - TILE], near], axis=0)
        top = jnp.max(near, axis=0, keepdims=True)
        powers = jnp.exp2((near - top) * SCALE2)
        total = jnp.sum(powers, axis=0, keepdims=True)
        stats[0, head : head + 1, block * TILE : count] = top * SCALE2 + jnp.log2(total)
        return powers.astype(BF), 1.0 / total

    def gather(head, block, powers, share):
        count = (block + 1) * TILE
        lanes = slice(head * HEAD, (head + 1) * HEAD)
        core[lanes, block * TILE : count] = dot(values_t[lanes, :count], powers) * share

    scores = score(*tasks[0])
    waiting = None
    for n, task in enumerate(tasks):
        ahead = score(*tasks[n + 1]) if n + 1 < len(tasks) else None
        softened = soften(*task, scores)
        if waiting is not None:
            gather(*waiting)
        waiting = task + softened
        scores = ahead
    gather(*waiting)
    core_own[...] = core[:, pl.ds(here, half)].T.astype(BF)
    core_far[...] = core[:, pl.ds(there, half)].T.astype(BF)


def attend(index, place, tokens, got, gain, wq, wk, wv):
    _, half, width = tokens.shape
    full = 2 * half
    quads = width // QUAD
    column = ((width, QUAD), lambda p, s: (0, p))
    wide = ((full, width), BF, (full, QUAD), lambda p, s: (0, p))
    part = ((half, width), BF, (half, QUAD), lambda p, s: (0, p))
    return call(
        forward_kernel,
        "attend_forward",
        13,
        (quads,),
        [
            (tokens, (1, half, width), lambda p, s: (2 * s[0] + index, 0, 0)),
            whole(got),
            whole(gain),
            (wq, *column),
            (wk, *column),
            (wv, *column),
        ],
        [
            ((full, width), BF, (full, width), same(0, 0)),
            wide,
            wide,
            wide,
            part,
            part,
            ((quads, 8, full), F32, (1, 8, full), lambda p, s: (p, 0, 0)),
        ],
        [pltpu.VMEM((QUAD, full), F32)],
        [],
        place,
    )


def stream_of(place, r, tok, attended, gain, router, slots):
    slot = lax.rem(r + 2 * place[0], slots)
    stream = tok.astype(F32) + attended
    second = (normed(stream)[0] * gain).astype(BF)
    logits = jnp.where(slot < place[1], dot(second, router), -1e30)
    return stream, second, logits


def early_kernel(place, tok, c0, c1, c2, wo, gain, router, resid, seconds, logits):
    slots, rows, width = tok.shape
    attended = dot(jnp.concatenate([c0[...], c1[...], c2[...]], axis=0), wo[...])
    for r in range(slots - 1):
        slot = lax.rem(r + 2 * place[0], slots)
        resid[r], seconds[r], logits[r] = stream_of(
            place, r, tok[slot], attended[r * rows : (r + 1) * rows], gain[...], router[...], slots
        )


def mix_kernel(
    place, tok, cot, c3, seconds, logits, wo, gain, router, held, resid, merged, d_expert, gates
):
    slots, rows, width = cot.shape
    stream, second, logit = stream_of(
        place, slots - 1, tok[0], dot(c3[...], wo[...]), gain[...], router[...], slots
    )
    resid[0] = stream
    logits = [logits[r] for r in range(slots - 1)] + [logit]
    seconds = [seconds[r].astype(F32) for r in range(slots - 1)] + [second.astype(F32)]
    slot_of = [lax.rem(r + 2 * place[0], slots) for r in range(slots)]
    top = jnp.maximum(jnp.maximum(logits[0], logits[1]), jnp.maximum(logits[2], logits[3]))
    powers = [
        jnp.where(slot_of[r] < place[1], jnp.exp(logits[r] - top), 0.0) for r in range(slots)
    ]
    total = powers[0] + powers[1] + powers[2] + powers[3]
    weights = []
    for r in range(slots):
        gate = powers[r] / total
        gates[r] = gate
        weights.append(gate.astype(BF).astype(F32))
    for e in range(2):
        both = jnp.zeros((rows, width), F32)
        back = jnp.zeros((rows, width), F32)
        for r in range(slots):
            weight = weights[r][:, e : e + 1]
            both = both + weight * seconds[r]
            back = back + weight * cot[slot_of[r]].astype(F32)
        merged[e] = both.astype(BF)
        d_expert[e] = back.astype(BF)


def mix_early(place, tokens, cores, output_weight, gain, router):
    slots, half, width = tokens.shape
    rows = 128
    quad = ((slots, rows, width), lambda p, s: (0, p, 0))
    part = ((rows, width), lambda p, s: (p, 0))
    three = (slots - 1, rows, width)
    return call(
        early_kernel,
        "mix_early",
        6,
        (half // rows,),
        [(tokens, *quad)]
        + [(core, *part) for core in cores]
        + [whole(output_weight), whole(gain), whole(router)],
        [
            ((slots, half, width), F32, three, quad[1]),
            ((slots - 1, half, width), BF, three, quad[1]),
            ((slots - 1, half, 128), F32, (slots - 1, rows, 128), quad[1]),
        ],
        [],
        [],
        place,
    )


def mix(place, tokens, cotangent, core, early, output_weight, gain, router):
    slots, half, width = tokens.shape
    rows = 128
    resid, seconds, logits = early
    last = ((1, rows, width), lambda p, s: (lax.rem(slots - 1 + 2 * s[0], slots), p, 0))
    quad = ((slots, rows, width), lambda p, s: (0, p, 0))
    twin = ((2, half, width), BF, (2, rows, width), lambda p, s: (0, p, 0))
    inputs = [
        (tokens, *last),
        (cotangent, *quad),
        (core, (rows, width), lambda p, s: (p, 0)),
        (seconds, (slots - 1, rows, width), quad[1]),
        (logits, (slots - 1, rows, 128), quad[1]),
        whole(output_weight),
        whole(gain),
        whole(router),
    ]
    outputs = [
        (resid.shape, F32, (1, rows, width), lambda p, s: (slots - 1, p, 0)),
        twin,
        twin,
        ((slots, half, 128), F32, (slots, rows, 128), quad[1]),
    ]
    return pl.pallas_call(
        mix_kernel,
        grid_spec=pltpu.PrefetchScalarGridSpec(
            num_scalar_prefetch=1,
            grid=(half // rows,),
            in_specs=[pl.BlockSpec(b, i) for _, b, i in inputs]
            + [pl.BlockSpec(memory_space=pl.ANY)],
            out_specs=[pl.BlockSpec(b, i) for _, _, b, i in outputs],
        ),
        out_shape=[jax.ShapeDtypeStruct(shape, kind) for shape, kind, _, _ in outputs],
        input_output_aliases={1 + len(inputs): 0},
        compiler_params=params(LIMIT),
        cost_estimate=cost(6),
        name="mix",
    )(place, *[array for array, _, _ in inputs], resid)


def expert_kernel(
    per, place, merged, d_expert, w_in, w_out, out, d_merged, keep, give, acc, d_acc, rows_t
):
    step = pl.program_id(0)
    rows = merged[0]
    back = d_expert[0]
    width = back.shape[1]
    root = math.sqrt(2.0 / math.pi)
    parts = w_in.shape[2] // TILE
    many = width // per
    mine = place[2] == 0

    @pl.when(step == 0)
    def _():
        rows_t[...] = rows.T

    def spans(n):
        return slice(n * TILE, (n + 1) * TILE)

    def ahead(n):
        return dot(rows, w_in[0, :, spans(n)]), dot_nt(back, w_out[0, spans(n), :])

    def bend(u, d_hidden):
        square = u * u
        bent = jnp.tanh(u * (root + (root * 0.044715) * square))
        hidden = (0.5 * u * (1.0 + bent)).astype(BF)
        slope = 0.5 * (1.0 + bent) + (0.5 * u) * (1.0 - bent * bent) * (
            root + (3.0 * root * 0.044715) * square
        )
        return hidden, (d_hidden * slope).astype(BF)

    def spread(n, hidden, d_pre):
        to_out = dot(hidden.T, back)
        to_out = jnp.concatenate([to_out[:, :TILE], to_out[:, TILE:]], axis=0)
        to_in = dot(rows_t[...], d_pre)
        shape = (many, per, TILE)
        at = slice(n * many, (n + 1) * many)
        keep[at] = jnp.where(mine, to_in, to_out).astype(BF).reshape(shape)
        give[at] = jnp.where(mine, to_out, to_in).astype(BF).reshape(shape)
        return dot(hidden, w_out[0, spans(n), :]), dot_nt(d_pre, w_in[0, :, spans(n)])

    forth, down, waiting = 0.0, 0.0, None
    current = ahead(0)
    for n in range(parts):
        later = ahead(n + 1) if n + 1 < parts else None
        bent = bend(*current)
        if waiting is not None:
            pair = spread(*waiting)
            forth, down = forth + pair[0], down + pair[1]
        waiting = (n,) + bent
        current = later
    pair = spread(*waiting)
    forth, down = forth + pair[0], down + pair[1]

    @pl.when(step == 0)
    def _():
        acc[...] = forth
        d_acc[...] = down

    @pl.when(step == pl.num_programs(0) - 1)
    def _():
        out[...] = (acc[...] + forth).astype(BF)
        d_merged[...] = (d_acc[...] + down).astype(BF)


def expert(e, place, count, merged, d_expert, w_in, w_out, deps):
    _, rows, width = merged.shape
    hidden = w_in.shape[2]
    chunk = hidden // 2
    per = hidden // TILE * width // count
    one = ((1, rows, width), same(e, 0, 0))
    flat = ((rows, width), BF, (rows, width), same(0, 0))
    part = ((count, per, TILE), BF, (count // 2, per, TILE), lambda f, s: (f, 0, 0))
    return call(
        lambda *refs: expert_kernel(per, *refs),
        "expert",
        13,
        (2,),
        [
            (merged, *one),
            (d_expert, *one),
            (w_in, (1, width, chunk), lambda f, s: (e, 0, f)),
            (w_out, (1, chunk, width), lambda f, s: (e, f, 0)),
        ],
        [flat, flat, part, part],
        [
            pltpu.VMEM((rows, width), F32),
            pltpu.VMEM((rows, width), F32),
            pltpu.VMEM((width, rows), BF),
        ],
        deps,
        place,
    )


def low_kernel(
    place, resid, cot, gates, x0, x1, m0, m1, router, gain, d2, d3, d0, lows_out, g_router, g_gain
):
    slots, rows, width = resid.shape
    outs = [x0[...].astype(F32), x1[...].astype(F32)]
    downs = [m0[...].astype(F32), m1[...].astype(F32)]
    lane = lax.broadcasted_iota(jnp.int32, (rows, 128), 1)
    hats, inverses, seconds, d_gates = [], [], [], []
    for r in range(slots):
        slot = lax.rem(r + 2 * place[0], slots)
        hat, inverse = normed(resid[r])
        second = (hat * gain[...]).astype(BF)
        hats.append(hat)
        inverses.append(inverse)
        seconds.append(second)
        cotangent = cot[slot].astype(F32)
        second = second.astype(F32)
        columns = [
            jnp.sum(cotangent * outs[e] + downs[e] * second, axis=-1, keepdims=True)
            for e in range(2)
        ]
        d_gates.append(jnp.where(lane == 0, columns[0], jnp.where(lane == 1, columns[1], 0.0)))
    mean = sum(gates[r] * d_gates[r] for r in range(slots))
    lows = [(gates[r] * (d_gates[r] - mean)).astype(BF) for r in range(slots)]
    gain_sum = jnp.zeros((1, width), F32)
    for r in range(slots):
        low = lows[r].astype(F32)
        lows_out[r] = low
        if r != 1:
            d_rows, gain_part = resid_back(
                cot[lax.rem(r + 2 * place[0], slots)], gates[r], low, downs, router, gain,
                hats[r], inverses[r],
            )
            {2: d2, 3: d3, 0: d0}[r][...] = d_rows
            gain_sum = gain_sum + gain_part
    low_rows = jnp.concatenate(lows, axis=0).astype(F32).T[:8].astype(BF)
    router_sum = dot(low_rows, jnp.concatenate(seconds, axis=0))
    add_up(g_router, router_sum)
    add_up(g_gain, jnp.broadcast_to(gain_sum, (8, width)))


def add_up(ref, value):
    @pl.when(pl.program_id(0) == 0)
    def _():
        ref[...] = value

    @pl.when(pl.program_id(0) > 0)
    def _():
        ref[...] += value


def resid_back(cotangent, gate, low, downs, router, gain, hat, inverse):
    weight = gate.astype(BF).astype(F32)
    d_second = sum(
        weight[:, e : e + 1] * downs[e] + low[:, e : e + 1] * router[e : e + 1, :]
        for e in range(2)
    )
    d_stream = norm_back(d_second * gain[...], hat, inverse)
    d_rows = (cotangent.astype(F32) + d_stream).astype(BF)
    return d_rows, jnp.sum(d_second * hat, axis=0, keepdims=True)


def own_kernel(
    place, resid, cot, gates, lows, m0, m1, router, gain, c0, c1, c2, c3, d0, d2, d3, g_router,
    g_gain_far, d1, keep, give, g_gain, g_out,
):
    step = pl.program_id(0)
    width = resid.shape[2]
    downs = [m0[...].astype(F32), m1[...].astype(F32)]
    hat, inverse = normed(resid[0])
    d_rows, gain_part = resid_back(
        cot[0], gates[0], lows[0], downs, router, gain, hat, inverse
    )
    d1[...] = d_rows
    add_up(g_gain, jnp.broadcast_to(gain_part, (8, width)))
    cores = jnp.concatenate([c0[...], c1[...], c2[...], c3[...]], axis=0)
    rows = jnp.concatenate([d0[...], d_rows, d2[...], d3[...]], axis=0)
    total = dot(cores.T, rows)

    add_up(g_out, total)

    @pl.when(step == pl.num_programs(0) - 1)
    def _():
        mine = place[2] == 0
        low, high = g_out[:, :TILE], g_out[:, TILE:]
        line = lax.broadcasted_iota(jnp.int32, (8, width), 0)
        small = jnp.where(line < 2, g_router[...], 0.0)
        small = jnp.where(line == 2, g_gain_far[...] + g_gain[...], small)
        small = jnp.concatenate(
            [small[:, :TILE], small[:, TILE:], jnp.zeros((width - 16, TILE), F32)], axis=0
        )
        blank = jnp.zeros((width, TILE), F32)
        one = jnp.concatenate([jnp.where(mine, low, high), jnp.where(mine, small, blank)])
        two = jnp.concatenate([jnp.where(mine, high, low), jnp.where(mine, blank, small)])
        keep[...] = one.astype(BF)
        give[...] = two.astype(BF)


def output_kernel(place, resid, gates, x0, x1, output):
    slots = resid.shape[0]
    outs = [x0[...].astype(F32), x1[...].astype(F32)]
    for r in range(slots):
        slot = lax.rem(r + 2 * place[0], slots)
        weight = gates[r].astype(BF).astype(F32)
        output[slot] = (
            resid[r] + weight[:, 0:1] * outs[0] + weight[:, 1:2] * outs[1]
        ).astype(BF)


def blocks_of(slots, rows, width):
    return dict(
        quad=((slots, rows, width), lambda p, s: (0, p, 0)),
        other=((1, rows, width), lambda p, s: (1, p, 0)),
        our_other=((1, rows, width), lambda p, s: (2 * s[0] + 1, p, 0)),
        other_lanes=((1, rows, 128), lambda p, s: (1, p, 0)),
        lanes=((slots, rows, 128), lambda p, s: (0, p, 0)),
        part=((rows, width), lambda p, s: (p, 0)),
        eight=((8, width), same(0, 0)),
    )


def unmix_far(place, resid, cotangent, gates, outs, downs, router, gain, deps):
    slots, half, width = resid.shape
    b = blocks_of(slots, 128, width)
    return call(
        low_kernel,
        "unmix_far",
        9,
        (half // 128,),
        [(resid, *b["quad"]), (cotangent, *b["quad"]), (gates, *b["lanes"])]
        + [(value, *b["part"]) for value in (*outs, *downs)]
        + [whole(router), whole(gain)],
        [((half, width), BF, *b["part"])] * 3
        + [((slots, half, 128), F32, *b["lanes"])]
        + [((8, width), F32, *b["eight"])] * 2,
        [],
        deps,
        place,
    )


def unmix_own(
    place, resid, cotangent, gates, lows, downs, router, gain, cores, d_rows, g_router, gain_far, deps
):
    slots, half, width = resid.shape
    b = blocks_of(slots, 128, width)
    rest = ((2 * width, TILE), BF, (2 * width, TILE), same(0, 0))
    return call(
        own_kernel,
        "unmix_own",
        1,
        (half // 128,),
        [(resid, *b["other"]), (cotangent, *b["our_other"])]
        + [(value, *b["other_lanes"]) for value in (gates, lows)]
        + [(value, *b["part"]) for value in downs]
        + [whole(router), whole(gain)]
        + [(value, *b["part"]) for value in (*cores, *d_rows)]
        + [whole(g_router), whole(gain_far)],
        [((half, width), BF, *b["part"]), rest, rest],
        [pltpu.VMEM((8, width), F32), pltpu.VMEM((width, width), F32)],
        deps,
        place,
    )


def write_output(place, resid, gates, outs, deps):
    slots, half, width = resid.shape
    b = blocks_of(slots, 128, width)
    return call(
        output_kernel,
        "write_output",
        1,
        (half // 128,),
        [(resid, *b["quad"]), (gates, *b["lanes"])] + [(value, *b["part"]) for value in outs],
        [((slots, half, width), BF, *b["quad"])],
        [],
        deps,
        place,
    )[0]


def backward_kernel(
    place, d_own, d_got, query, keys, values, core_own, core_far, stats, wo, three,
    d_attn, core, dq_t, d_keys, d_values,
):
    half = d_own.shape[0]
    full = 2 * half
    here = pl.multiple_of(place[0] * half, half)
    there = pl.multiple_of((1 - place[0]) * half, half)
    d_attn[pl.ds(here, half), :] = d_own[...]
    d_attn[pl.ds(there, half), :] = d_got[...]
    core[pl.ds(here, half), :] = core_own[...]
    core[pl.ds(there, half), :] = core_far[...]
    d_core = dot_nt(d_attn[...], wo[...]).astype(BF)
    product = (d_core.astype(F32) * core[...].astype(F32)).T
    masks = lane_masks(BF)
    keys_t = keys[...].T
    causal = causal_tile()
    tasks = [
        (head, block) for head in range(query.shape[1] // HEAD) for block in range(full // TILE)
    ]

    def of_pair(head):
        return slice(head // 2 * PAIR, (head // 2 + 1) * PAIR)

    def score(head, block):
        pair, mask, count = of_pair(head), masks[head % 2], (block + 1) * TILE
        span = slice(block * TILE, count)
        scores = dot_nt(keys[:count, pair] * mask, query[span, pair])
        d_probs = dot_nt(values[:count, pair] * mask, d_core[span, pair])
        return scores, d_probs

    def soften(head, block, scores, d_probs):
        count = (block + 1) * TILE
        span = slice(block * TILE, count)
        delta = jnp.sum(product[head * HEAD : (head + 1) * HEAD, span], axis=0, keepdims=True)
        probs = jnp.exp2(scores * SCALE2 - stats[0, head : head + 1, span])
        near = jnp.where(causal, probs[count - TILE :], 0.0)
        if block > 0:
            near = jnp.concatenate([probs[: count - TILE], near], axis=0)
        return near.astype(BF), (near * (d_probs - delta)).astype(BF)

    def spread(head, block, probs, d_scores):
        pair, mask, count = of_pair(head), masks[head % 2], (block + 1) * TILE
        span, before = slice(block * TILE, count), slice(0, count - TILE)
        lanes = slice(head * HEAD, (head + 1) * HEAD)
        to_value = dot(probs, d_core[span, pair] * mask)
        to_key = dot(d_scores, query[span, pair] * mask)
        if head % 2 == 0:
            d_values[span, pair] = to_value[count - TILE :]
            d_keys[span, pair] = to_key[count - TILE :]
            if block > 0:
                d_values[before, pair] += to_value[before]
                d_keys[before, pair] += to_key[before]
        else:
            d_values[:count, pair] += to_value
            d_keys[:count, pair] += to_key
        dq_t[lanes, span] = dot(keys_t[lanes, :count], d_scores)

    scored = score(*tasks[0])
    waiting = None
    for n, task in enumerate(tasks):
        ahead = score(*tasks[n + 1]) if n + 1 < len(tasks) else None
        softened = soften(*task, *scored)
        if waiting is not None:
            spread(*waiting)
        waiting = task + softened
        scored = ahead
    spread(*waiting)
    three[:, :QUAD] = (dq_t[...].T * SCALE).astype(BF)
    three[:, QUAD : 2 * QUAD] = (d_keys[...] * SCALE).astype(BF)
    three[:, 2 * QUAD :] = d_values[...].astype(BF)


def attend_back(us, quads, place, d_own, d_got, kept, wo, deps):
    first, query, keys, values, core_own, core_far, stats = kept
    half, width = d_own.shape
    full = 2 * half
    start, count = quads

    def column(rows):
        return (rows, QUAD), lambda p, s: (0, start + p)

    return call(
        backward_kernel,
        "attend_backward",
        us,
        (count,),
        [
            whole(d_own),
            whole(d_got),
            (query, *column(full)),
            (keys, *column(full)),
            (values, *column(full)),
            (core_own, *column(half)),
            (core_far, *column(half)),
            (stats, (1, 8, full), lambda p, s: (start + p, 0, 0)),
            (wo, (QUAD, width), lambda p, s: (start + p, 0)),
        ],
        [((full, count * 3 * QUAD), BF, (full, 3 * QUAD), lambda p, s: (0, p))],
        [
            pltpu.VMEM((full, width), BF),
            pltpu.VMEM((full, QUAD), BF),
            pltpu.VMEM((QUAD, full), F32),
            pltpu.VMEM((full, QUAD), F32),
            pltpu.VMEM((full, QUAD), F32),
        ],
        deps,
        place,
    )[0]


def first_kernel(place, t0, t1, own, got, gain, wq, wk, wv, d_tok_own, d_tok_far):
    d_first = 0.0
    for quad, three in enumerate((t0, t1)):
        lanes = slice(quad * QUAD, (quad + 1) * QUAD)
        weights = [w[:, lanes] for w in (wq, wk, wv)]
        d_first = d_first + dot_nt(three[...], jnp.concatenate(weights, axis=1))
    near = pl.program_id(0) == 0
    value = jnp.where(near, own[0].astype(F32), got[...].astype(F32))
    hat, inverse = normed(value)
    result = norm_back(d_first * gain[...], hat, inverse).astype(BF)

    @pl.when(near)
    def _():
        d_tok_own[...] = result

    @pl.when(jnp.logical_not(near))
    def _():
        d_tok_far[...] = result


def first_back(us, index, place, threes, tokens, got, gain, weights, deps):
    _, half, width = tokens.shape
    rows = 256
    blocks = half // rows

    def row_block(h, j, s):
        return jnp.where(h == 0, s[0], 1 - s[0]) * blocks + j

    return call(
        first_kernel,
        "first_back",
        us,
        (2, blocks),
        [
            (three, (rows, 3 * QUAD), lambda h, j, s, c=c: (row_block(h, j, s), c))
            for three, c in threes
        ]
        + [
            (
                tokens,
                (1, rows, width),
                lambda h, j, s: (2 * s[0] + index, jnp.where(h == 0, j, blocks - 1), 0),
            ),
            (got, (rows, width), lambda h, j, s: (jnp.where(h == 0, 0, j), 0)),
            whole(gain),
            *[whole(weight) for weight in weights],
        ],
        [
            (
                (half, width),
                BF,
                (rows, width),
                lambda h, j, s: (jnp.where(h == 0, j, blocks - 1), 0),
            ),
            ((half, width), BF, (rows, width), lambda h, j, s: (jnp.where(h == 0, 0, j), 0)),
        ],
        [],
        deps,
        place,
    )


def early_project_kernel(place, first, low_three, high_three, low, high):
    low[...] = dot_tn(first[...], low_three[...])
    high[...] = dot_tn(first[...], high_three[...])


def project_kernel(place, first, low_three, high_three, low, high, keep, give):
    mine = place[2] == 0
    low_sum = low[...] + dot_tn(first[...], low_three[...])
    high_sum = high[...] + dot_tn(first[...], high_three[...])
    keep[...] = jnp.where(mine, low_sum, high_sum).astype(BF)
    give[...] = jnp.where(mine, high_sum, low_sum).astype(BF)


def project_grads(place, first, threes, earlier, deps):
    full, width = first.shape
    block = ((width, QUAD), lambda p, s: (p, 0))
    out = ((3 * width, QUAD), BF if earlier else F32, *block)
    return call(
        project_kernel if earlier else early_project_kernel,
        "project_grads",
        1,
        (3,),
        [whole(first)]
        + [(three, (full, QUAD), lambda p, s, c=c: (0, 3 * c + p)) for three, c in threes]
        + [(value, *block) for value in earlier],
        [out, out],
        [],
        deps,
        place,
    )


def chip_bits(devices):
    return [1] + [1 << n for n in range(2, devices.bit_length() - 1)]


def masks_of(level):
    return [level[0], level[1], level[0] + level[1]] if len(level) > 1 else [level[0]]


def send(value, mask, devices):
    return lax.ppermute(value, AXES, [(n, n ^ mask) for n in range(devices)])


class Summed:
    def __init__(self, lanes, devices, levels, lane_levels):
        self.devices, self.levels, self.lane_levels = devices, levels, lane_levels
        self.steps, self.count, self.parts = 0, len(levels), None
        self.arrays, self.orders, self.rows = [], [], []
        for lane, own in zip(lanes, lane_levels):
            self.arrays += [[keep, send(give, 2, devices)] for keep, give in lane]
            order = own[0] if len(own) == 1 else [bit for level in reversed(own) for bit in level]
            self.orders += [order] * len(lane)
            self.rows.append(sum(keep.shape[1] for keep, _ in lane))

    def jobs(self):
        n = self.steps
        if n == 0:
            return [(self.arrays, self.levels[0], self.orders)]
        if n <= self.count:
            level = self.levels[n] if n < self.count else []
            return [(self.arrays, level, [level] * len(self.arrays))]
        if self.parts is not None:
            return [(part, None, [part[0][0].shape[1]]) for part in self.parts]
        return [(self.arrays, None, self.rows if n == 2 * self.count - 1 else [sum(self.rows)])]

    def take(self, results):
        n, count = self.steps, self.count
        self.steps += 1
        if n < count:
            mine, *others = results[0]
            masks = masks_of(self.levels[n])
            got = [send(other, mask, self.devices) for other, mask in zip(others, masks)]
            self.arrays = [[mine] + got]
            return
        values = [value for result in results for value in result]
        if n < 2 * count - 1:
            masks = masks_of(self.levels[2 * count - 1 - n])
            self.arrays = [values + [send(values[0], mask, self.devices) for mask in masks]]
            return
        self.parts = []
        for own, value in zip(self.lane_levels, values):
            masks = masks_of(own[len(own) - 1 - (n - 2 * count + 1)])
            self.parts.append([[value] + [send(value, mask, self.devices) for mask in masks]])

    def done(self):
        return self.steps >= 2 * self.count - 1 + len(self.lane_levels[0])

    def exchange(self):
        self.early = [send(part[0][0], 2, self.devices) for part in self.parts]
        return self.early

    def finish(self):
        return [
            part[0] + [first] + [send(some, 2, self.devices) for some in part[0][1:]]
            for part, first in zip(self.parts, self.early)
        ]


def step_kernel(kinds, place, *refs):
    ins = sum(sum(groups) for _, groups, _ in kinds)
    inputs, outputs = refs[:ins], refs[ins:]
    for adds, groups, n_out in kinds:
        here, inputs = inputs[: sum(groups)], inputs[sum(groups) :]
        there, outputs = outputs[:n_out], outputs[n_out:]
        if not adds:
            size, row = here[0].shape[0], 0
            for target in there:
                rows = target.shape[1]
                for n, ref in enumerate(here):
                    target[n * size : (n + 1) * size] = ref[:, row : row + rows, :]
                row += rows
            continue
        for target in there:
            row = 0
            for each in groups[: len(groups) // n_out]:
                total = here[0][...].astype(F32)
                for other in here[1:each]:
                    total = total + other[...].astype(F32)
                here, rows = here[each:], total.shape[1]
                target[:, row : row + rows, :] = total.astype(BF)
                row += rows


def advance(chains, place, deps, us=3):
    jobs = [chain.jobs() for chain in chains]
    every = [job for some in jobs for job in some]
    splits = [arrays[0][0].shape[0] >> len(level or []) for arrays, level, _ in every]
    big = max(array[0].size for arrays, _, _ in every for array in arrays)
    steps = max(1, 4 * big // MIB) if all(level is not None for _, level, _ in every) else 1
    steps = min([steps] + splits)
    inputs, outputs, kinds = [], [], []
    for (arrays, level, orders), split in zip(every, splits):
        width = arrays[0][0].shape[2]
        if level is None:
            count = split * len(arrays[0])
            inputs += [whole(array) for array in arrays[0]]
            for rows in orders:
                shape = (count, rows, width)
                outputs.append((shape, BF, shape, lambda p, s: (0, 0, 0)))
            kinds.append((False, [len(arrays[0])], len(orders)))
            continue
        block = split // steps
        rows = sum(some[0].shape[1] for some in arrays)

        def index(mask, order):
            def at(p, s):
                own = 0
                for n, bit in enumerate(order):
                    own = own + (lax.rem(s[4] // bit + (1 if mask & bit else 0), 2) << n)
                return (own * steps + p, 0, 0)

            return at

        for mask in [0] + (masks_of(level) if level else []):
            for some, order in zip(arrays, orders):
                inputs += [(a, (block,) + a.shape[1:], index(mask, order)) for a in some]
            outputs.append(
                ((split, rows, width), BF, (block, rows, width), lambda p, s: (p, 0, 0))
            )
        n_out = 1 << len(level)
        kinds.append((True, [len(some) for some in arrays] * n_out, n_out))
    results = call(
        lambda *refs: step_kernel(kinds, *refs), "sum_step", us, (steps,), inputs, outputs, [],
        deps, place,
    )
    mark, groups = results[0], []
    for _, _, n_out in kinds:
        groups.append(results[:n_out])
        results = results[n_out:]
    for chain, some in zip(chains, jobs):
        chain.take(groups[: len(some)])
        groups = groups[len(some) :]
    return [mark]


def result_kernel(per, each, experts, place, *refs):
    held, (grad_in, grad_out) = refs[:-2], refs[-2:]
    mine = place[2] == 0
    half = each // 2
    for n, e in enumerate(experts):

        @pl.when(pl.program_id(0) == n)
        def _():
            own, other = held[2 * n : 2 * n + 2]
            swap = place[3 + 2 * e] & (each - 1)
            for t in range(each):
                first, second = own[t ^ swap].astype(F32), other[t ^ swap].astype(F32)
                low, high = jnp.where(mine, first, second), jnp.where(mine, second, first)
                grad_in[0, t * per : (t + 1) * per, :] = low
                lanes = slice(t // half * TILE, (t // half + 1) * TILE)
                grad_out[0, t % half * per : (t % half + 1) * per, lanes] = high


def expert_results(experts, d, place, parts, width, hidden, per, earlier, deps):
    inner = parts[0][0].shape[0]
    each = width // per
    blocks = inner // each

    def chip(e, s):
        return s[3 + 2 * e]

    def expert(n):
        return n + experts[0]

    def piece(n, k, s):
        some = jnp.where(expert(n) == 0, s[3], s[5])
        return (d ^ (some // inner)) * blocks + k

    def part_index(own):
        def index(n, k, s):
            e, first = expert(n), (chip(own, s) % inner) // each
            at = jnp.where(e == own, k, jnp.where(e < own, 0, blocks - 1))
            return (at ^ first, 0, 0)

        return index

    inputs = []
    for e in experts:
        inputs += [
            (parts[e][n], (each, per, TILE), part_index(e)) for n in (d, len(parts[e]) // 2 + d)
        ]
    outputs = [
        ((2, width, hidden), F32, (1, width, TILE), lambda n, k, s: (expert(n), 0, piece(n, k, s))),
        ((2, hidden, width), F32, (1, TILE, width), lambda n, k, s: (expert(n), piece(n, k, s), 0)),
    ]
    any_ref = pl.BlockSpec(memory_space=pl.ANY)
    held = len(earlier) + len(deps)

    def body(place_ref, *refs):
        result_kernel(per, each, experts, place_ref, *refs[held:])

    return pl.pallas_call(
        body,
        grid_spec=pltpu.PrefetchScalarGridSpec(
            num_scalar_prefetch=1,
            grid=(len(experts), blocks),
            in_specs=[any_ref] * held + [pl.BlockSpec(b, i) for _, b, i in inputs],
            out_specs=[pl.BlockSpec(b, i) for _, _, b, i in outputs],
        ),
        out_shape=[jax.ShapeDtypeStruct(shape, kind) for shape, kind, _, _ in outputs],
        input_output_aliases={1 + n: n for n in range(len(earlier))},
        compiler_params=params(LIMIT, "arbitrary", "arbitrary"),
        cost_estimate=cost(5 * len(experts)),
        name="expert_results",
    )(place, *earlier, *deps, *[array for array, _, _ in inputs])


def project_result_kernel(place, *refs):
    count = (len(refs) - 13) // 2
    parts, others = refs[:count], refs[count : 2 * count]
    weights, gain = refs[2 * count : 2 * count + 3], refs[2 * count + 3]
    grads = refs[2 * count + 4 : 2 * count + 8]
    g_gain, g_gain2, g_router, halves, rest = refs[2 * count + 8 :]
    inner, rows, _ = parts[0].shape
    width = gain.shape[1]
    per = 3 * width // (count * inner)
    for d in range(count):
        for m in range(inner):
            shard = (d * inner + m) ^ place[3]
            at = pl.ds(pl.multiple_of(shard * per, 8), per)
            more = pl.ds(pl.multiple_of(shard * (rows - per), 8), rows - per)
            for half, source in ((place[2], parts), (1 - place[2], others)):
                value = source[d][m].astype(F32)
                halves[half, at, :] = value[:per]
                rest[half, more, :] = value[per:]
    total = jnp.zeros((width, 1), F32)
    for n in range(4):
        for h in range(2):
            lanes = slice(h * QUAD, (h + 1) * QUAD)
            if n == 3:
                grads[n][:, lanes] = rest[h, :width, :]
                continue
            value = halves[h, n * width : (n + 1) * width, :]
            grads[n][:, lanes] = value
            total += jnp.sum(value * weights[n][:, lanes].astype(F32), axis=1, keepdims=True)
    g_gain[...] = jnp.broadcast_to(total, (width, 128)).T[:1] / gain[...]
    for h in range(2):
        lanes = slice(h * QUAD, (h + 1) * QUAD)
        small = rest[0, width + 8 * h : width + 8 * (h + 1), :]
        g_router[:, lanes] = small[:2]
        g_gain2[:, lanes] = small[2:3]


def project_result(place, chip, parts, weights, gain, deps):
    width = gain.shape[1]
    square = ((width, width), F32, (width, width), same(0, 0))
    line = ((1, width), F32, (1, width), same(0, 0))
    return call(
        project_result_kernel,
        "project_result",
        1,
        (1,),
        [whole(value) for value in (*parts, *weights, gain)],
        [square] * 4 + [line, line, ((2, width), F32, (2, width), same(0, 0))],
        [pltpu.VMEM((2, 3 * width, QUAD), F32), pltpu.VMEM((2, 2 * width, QUAD), F32)],
        deps,
        place.at[3].set(chip),
    )


def shards(
    tokens, seq_counts, norm1_gain, w_query, w_key, w_value, output_weight, norm2_gain,
    router_weight, w_expert_in, w_expert_out, cotangent,
):
    slots, half, width = tokens.shape
    hidden = w_expert_in.shape[2]
    devices = lax.axis_size("dp") * lax.axis_size("blk")
    count = devices // 2
    blk = lax.axis_index("blk")
    dp = lax.axis_index("dp")
    me = dp * 2 + blk
    core_bit = lax.rem(dp, 2)
    bits = chip_bits(devices)
    x, y, *more = bits
    levels = [bits[n : n + 2] for n in range(0, len(bits), 2)]
    lanes = [[[y], [x]], [[x], [y]]]

    def chip_of(levels):
        chip = jnp.int32(0)
        for level in levels:
            for bit in reversed(level):
                chip = chip * 2 + lax.rem(me // bit, 2)
        return chip

    place = jnp.stack([blk, seq_counts[0], core_bit, jnp.int32(0), me]).astype(jnp.int32)
    gain1 = norm1_gain.reshape(1, width)
    gain2 = norm2_gain.reshape(1, width)
    router = jnp.pad(router_weight, ((0, 0), (0, 126)))
    router_rows = jnp.pad(router_weight.T.astype(F32), ((0, 6), (0, 0)))
    weights = (w_query, w_key, w_value)

    def swap(value):
        return send(value, 1, devices)

    far = [
        lax.dynamic_index_in_dim(tokens, lax.rem(2 + i + 2 * blk, 4), 0, keepdims=False)
        for i in range(2)
    ]
    got = [swap(value) for value in far]
    kept = [
        attend(i, place, tokens, got[i], gain1, w_query, w_key, w_value) for i in range(2)
    ]
    cores = [kept[0][4], kept[1][4], swap(kept[0][5]), swap(kept[1][5])]
    early = mix_early(place, tokens, cores[:3], output_weight, gain2, router)
    resid, merged, d_expert, gates = mix(
        place, tokens, cotangent, cores[3], early, output_weight, gain2, router
    )
    per = hidden // TILE * width // count
    done = [expert(0, place, count, merged, d_expert, w_expert_in, w_expert_out, [])]
    done.append(
        expert(1, place, count, merged, d_expert, w_expert_in, w_expert_out, [done[0][0]])
    )
    outs, downs = [d[0] for d in done], [d[1] for d in done]
    summed = Summed([[done[0][2:4]], [done[1][2:4]]], devices, levels, lanes)
    d2, d3, d0, lows, g_router, gain_far = unmix_far(
        place, resid, cotangent, gates, outs, downs, router_rows, gain2, []
    )
    d_got = [swap(d2), swap(d3)]
    marks = advance([summed], place, [d2])

    a0 = attend_back(15, (0, 1), place, d0, d_got[0], kept[0], output_weight, marks)
    a1 = attend_back(15, (1, 1), place, d0, d_got[0], kept[0], output_weight, [a0])
    d1, *rest = unmix_own(
        place, resid, cotangent, gates, lows, downs, router_rows, gain2, cores, [d0, d2, d3],
        g_router, gain_far, [a1],
    )
    rest = [value.reshape(count, -1, TILE) for value in rest]
    threes = [[(a0, 0), (a1, 0)]]
    far_a = first_back(1, 0, place, threes[0], tokens, got[0], gain1, weights, [d1, d_got[1]])
    t_far = [swap(far_a[1])]

    def back(quad, us, deps):
        return attend_back(us, (quad, 1), place, d1, d_got[1], kept[1], output_weight, deps)

    b0 = back(0, 1, [far_a[0]])
    early = project_grads(place, kept[0][0], threes[0], [], [b0])
    b1 = back(1, 20, [t_far[0]] + advance([summed], place, [early[0]]))
    threes.append([(b0, 0), (b1, 0)])
    pair = project_grads(place, kept[1][0], threes[1], early, [b1])
    pair = [value.reshape(count, -1, QUAD) for value in pair]
    last = Summed([[pair, rest]], devices, levels, [levels[:1]])
    marks = advance([summed], place, [pair[0]])
    marks = advance([last], place, marks)
    far_b = first_back(6, 1, place, threes[1], tokens, got[1], gain1, weights, marks)
    t_far.append(swap(far_b[1]))
    marks = advance([summed, last], place, [far_b[0]])
    output = write_output(place, resid, gates, outs, marks)
    marks = advance([last], place, [output], 1)
    while not summed.done():
        marks = advance([summed], place, marks + [t_far[1]], 1)
    marks = marks + summed.exchange()
    while not last.done():
        marks = advance([last], place, marks, 1)
    last.exchange()
    own = [
        (d.astype(F32) + t.astype(F32)).astype(BF)
        for d, t in zip((d0, d1), (far_a[0], far_b[0]))
    ]
    other = [(d.astype(F32) + t.astype(F32)).astype(BF) for d, t in zip((d2, d3), t_far)]
    grad_tokens = jnp.where(blk == 0, jnp.stack(own + other), jnp.stack(other + own))
    parts = summed.finish()
    chips = [chip_of(lane + levels[1:]) for lane in lanes]
    final = jnp.stack([blk, seq_counts[0], core_bit, chips[0], me, chips[1]]).astype(jnp.int32)
    results = []
    for e in range(2):
        results = expert_results((e,), 0, final, parts, width, hidden, per, results, [])
    grad_in, grad_out = expert_results(
        (0, 1), 1, final, parts, width, hidden, per, results, []
    )
    *grads, grad_gain1, grad_gain2, grad_router = project_result(
        place, chip_of(levels), last.finish()[0], weights, gain1, [grad_in]
    )
    return (
        output, grad_tokens, grad_gain1.reshape(width), *grads, grad_gain2.reshape(width),
        grad_router.T, grad_in, grad_out,
    )


def solution(mesh):
    data = P("dp", "blk", None)
    return jax.shard_map(
        shards,
        mesh=mesh,
        in_specs=(data, P("dp")) + (P(),) * 9 + (data,),
        out_specs=(data, data) + (P(),) * 9,
        check_vma=False,
    )
```

```python
import math

import jax
import jax.numpy as jnp
from jax import lax
from jax.experimental import pallas as pl
from jax.experimental.pallas import tpu as pltpu
from jax.sharding import PartitionSpec as P

HEADS = 8
HEAD = 64
PAIR = 2 * HEAD
QUAD = 4 * HEAD
EPS = 1e-05
SCALE = HEAD ** (-0.5)
SCALE2 = SCALE * math.log2(math.e)
TILE = 256
BF = jnp.bfloat16
F32 = jnp.float32
AXES = ("dp", "blk")
MIB = 1 << 20
LIMIT = 64
FLOPS = 2_000_000_000


def dot(left, right):
    return jnp.dot(left, right, preferred_element_type=F32)


def dot_nt(left, right):
    return lax.dot_general(left, right, (((1,), (1,)), ((), ())), preferred_element_type=F32)


def dot_tn(left, right):
    return lax.dot_general(left, right, (((0,), (0,)), ((), ())), preferred_element_type=F32)


def normed(value):
    center = value - jnp.mean(value, axis=-1, keepdims=True)
    inverse = lax.rsqrt(jnp.mean(center * center, axis=-1, keepdims=True) + EPS)
    return center * inverse, inverse


def norm_back(scaled, hat, inverse):
    return inverse * (
        scaled
        - jnp.mean(scaled, axis=-1, keepdims=True)
        - hat * jnp.mean(scaled * hat, axis=-1, keepdims=True)
    )


def lane_masks(dtype):
    lane = lax.broadcasted_iota(jnp.int32, (1, PAIR), 1)
    low = (lane < HEAD).astype(F32)
    return low.astype(dtype), (1.0 - low).astype(dtype)


def causal_tile():
    shape = (TILE, TILE)
    return lax.broadcasted_iota(jnp.int32, shape, 0) <= lax.broadcasted_iota(jnp.int32, shape, 1)


def params(limit, *semantics):
    return pltpu.CompilerParams(
        vmem_limit_bytes=limit * MIB, dimension_semantics=semantics or ("arbitrary",)
    )


def cost(us):
    return pl.CostEstimate(flops=int(us * FLOPS), bytes_accessed=1000, transcendentals=0)


def call(kernel, name, us, grid, inputs, outputs, scratch, deps, place):
    any_ref = pl.BlockSpec(memory_space=pl.ANY)

    def body(place_ref, *refs):
        kernel(place_ref, *refs[len(deps) :])

    return pl.pallas_call(
        body,
        grid_spec=pltpu.PrefetchScalarGridSpec(
            num_scalar_prefetch=1,
            grid=grid,
            in_specs=[any_ref] * len(deps) + [pl.BlockSpec(b, i) for _, b, i in inputs],
            out_specs=[pl.BlockSpec(b, i) for _, _, b, i in outputs],
            scratch_shapes=scratch,
        ),
        out_shape=[jax.ShapeDtypeStruct(shape, kind) for shape, kind, _, _ in outputs],
        compiler_params=params(LIMIT, *["arbitrary"] * len(grid)),
        cost_estimate=cost(us),
        name=name,
    )(place, *deps, *[array for array, _, _ in inputs])


def whole(array):
    zeros = (0,) * array.ndim
    return array, array.shape, lambda *_: zeros


def same(*index):
    return lambda step, *_: index


def forward_kernel(
    place, tok, got, gain, wq, wk, wv, first, query, keys, values, core_own, core_far, stats, core
):
    half = got.shape[0]
    full = 2 * half
    here = pl.multiple_of(place[0] * half, half)
    there = pl.multiple_of((1 - place[0]) * half, half)

    @pl.when(pl.program_id(0) == 0)
    def _():
        first[pl.ds(here, half), :] = (normed(tok[0].astype(F32))[0] * gain[...]).astype(BF)
        first[pl.ds(there, half), :] = (normed(got[...].astype(F32))[0] * gain[...]).astype(BF)

    rows = first[...]
    query[...] = dot(rows, wq[...]).astype(BF)
    keys[...] = dot(rows, wk[...]).astype(BF)
    values[...] = dot(rows, wv[...]).astype(BF)
    masks = lane_masks(BF)
    values_t = values[...].T
    causal = causal_tile()
    tasks = [
        (head, block) for head in range(query.shape[1] // HEAD) for block in range(full // TILE)
    ]

    def score(head, block):
        pair = slice(head // 2 * PAIR, (head // 2 + 1) * PAIR)
        count = (block + 1) * TILE
        key_half = keys[:count, pair] * masks[head % 2]
        return dot_nt(key_half, query[block * TILE : count, pair])

    def soften(head, block, scores):
        count = (block + 1) * TILE
        near = jnp.where(causal, scores[count - TILE :], -1e30)
        if block > 0:
            near = jnp.concatenate([scores[: count - TILE], near], axis=0)
        top = jnp.max(near, axis=0, keepdims=True)
        powers = jnp.exp2((near - top) * SCALE2)
        total = jnp.sum(powers, axis=0, keepdims=True)
        stats[0, head : head + 1, block * TILE : count] = top * SCALE2 + jnp.log2(total)
        return powers.astype(BF), 1.0 / total

    def gather(head, block, powers, share):
        count = (block + 1) * TILE
        lanes = slice(head * HEAD, (head + 1) * HEAD)
        core[lanes, block * TILE : count] = dot(values_t[lanes, :count], powers) * share

    scores = score(*tasks[0])
    waiting = None
    for n, task in enumerate(tasks):
        ahead = score(*tasks[n + 1]) if n + 1 < len(tasks) else None
        softened = soften(*task, scores)
        if waiting is not None:
            gather(*waiting)
        waiting = task + softened
        scores = ahead
    gather(*waiting)
    core_own[...] = core[:, pl.ds(here, half)].T.astype(BF)
    core_far[...] = core[:, pl.ds(there, half)].T.astype(BF)


def attend(index, place, tokens, got, gain, wq, wk, wv):
    _, half, width = tokens.shape
    full = 2 * half
    quads = width // QUAD
    column = ((width, QUAD), lambda p, s: (0, p))
    wide = ((full, width), BF, (full, QUAD), lambda p, s: (0, p))
    part = ((half, width), BF, (half, QUAD), lambda p, s: (0, p))
    return call(
        forward_kernel,
        "attend_forward",
        13,
        (quads,),
        [
            (tokens, (1, half, width), lambda p, s: (2 * s[0] + index, 0, 0)),
            whole(got),
            whole(gain),
            (wq, *column),
            (wk, *column),
            (wv, *column),
        ],
        [
            ((full, width), BF, (full, width), same(0, 0)),
            wide,
            wide,
            wide,
            part,
            part,
            ((quads, 8, full), F32, (1, 8, full), lambda p, s: (p, 0, 0)),
        ],
        [pltpu.VMEM((QUAD, full), F32)],
        [],
        place,
    )


def stream_of(place, r, tok, attended, gain, router, slots):
    slot = lax.rem(r + 2 * place[0], slots)
    stream = tok.astype(F32) + attended
    second = (normed(stream)[0] * gain).astype(BF)
    logits = jnp.where(slot < place[1], dot(second, router), -1e30)
    return stream, second, logits


def early_kernel(place, tok, c0, c1, c2, wo, gain, router, resid, seconds, logits):
    slots, rows, width = tok.shape
    attended = dot(jnp.concatenate([c0[...], c1[...], c2[...]], axis=0), wo[...])
    for r in range(slots - 1):
        slot = lax.rem(r + 2 * place[0], slots)
        resid[r], seconds[r], logits[r] = stream_of(
            place, r, tok[slot], attended[r * rows : (r + 1) * rows], gain[...], router[...], slots
        )


def mix_kernel(
    place, tok, cot, c3, seconds, logits, wo, gain, router, held, resid, merged, d_expert, gates
):
    slots, rows, width = cot.shape
    stream, second, logit = stream_of(
        place, slots - 1, tok[0], dot(c3[...], wo[...]), gain[...], router[...], slots
    )
    resid[0] = stream
    logits = [logits[r] for r in range(slots - 1)] + [logit]
    seconds = [seconds[r].astype(F32) for r in range(slots - 1)] + [second.astype(F32)]
    slot_of = [lax.rem(r + 2 * place[0], slots) for r in range(slots)]
    top = jnp.maximum(jnp.maximum(logits[0], logits[1]), jnp.maximum(logits[2], logits[3]))
    powers = [
        jnp.where(slot_of[r] < place[1], jnp.exp(logits[r] - top), 0.0) for r in range(slots)
    ]
    total = powers[0] + powers[1] + powers[2] + powers[3]
    weights = []
    for r in range(slots):
        gate = powers[r] / total
        gates[r] = gate
        weights.append(gate.astype(BF).astype(F32))
    for e in range(2):
        both = jnp.zeros((rows, width), F32)
        back = jnp.zeros((rows, width), F32)
        for r in range(slots):
            weight = weights[r][:, e : e + 1]
            both = both + weight * seconds[r]
            back = back + weight * cot[slot_of[r]].astype(F32)
        merged[e] = both.astype(BF)
        d_expert[e] = back.astype(BF)


def mix_early(place, tokens, cores, output_weight, gain, router):
    slots, half, width = tokens.shape
    rows = 128
    quad = ((slots, rows, width), lambda p, s: (0, p, 0))
    part = ((rows, width), lambda p, s: (p, 0))
    three = (slots - 1, rows, width)
    return call(
        early_kernel,
        "mix_early",
        6,
        (half // rows,),
        [(tokens, *quad)]
        + [(core, *part) for core in cores]
        + [whole(output_weight), whole(gain), whole(router)],
        [
            ((slots, half, width), F32, three, quad[1]),
            ((slots - 1, half, width), BF, three, quad[1]),
            ((slots - 1, half, 128), F32, (slots - 1, rows, 128), quad[1]),
        ],
        [],
        [],
        place,
    )


def mix(place, tokens, cotangent, core, early, output_weight, gain, router):
    slots, half, width = tokens.shape
    rows = 256
    resid, seconds, logits = early
    last = ((1, rows, width), lambda p, s: (lax.rem(slots - 1 + 2 * s[0], slots), p, 0))
    quad = ((slots, rows, width), lambda p, s: (0, p, 0))
    twin = ((2, half, width), BF, (2, rows, width), lambda p, s: (0, p, 0))
    inputs = [
        (tokens, *last),
        (cotangent, *quad),
        (core, (rows, width), lambda p, s: (p, 0)),
        (seconds, (slots - 1, rows, width), quad[1]),
        (logits, (slots - 1, rows, 128), quad[1]),
        whole(output_weight),
        whole(gain),
        whole(router),
    ]
    outputs = [
        (resid.shape, F32, (1, rows, width), lambda p, s: (slots - 1, p, 0)),
        twin,
        twin,
        ((slots, half, 128), F32, (slots, rows, 128), quad[1]),
    ]
    return pl.pallas_call(
        mix_kernel,
        grid_spec=pltpu.PrefetchScalarGridSpec(
            num_scalar_prefetch=1,
            grid=(half // rows,),
            in_specs=[pl.BlockSpec(b, i) for _, b, i in inputs]
            + [pl.BlockSpec(memory_space=pl.ANY)],
            out_specs=[pl.BlockSpec(b, i) for _, _, b, i in outputs],
        ),
        out_shape=[jax.ShapeDtypeStruct(shape, kind) for shape, kind, _, _ in outputs],
        input_output_aliases={1 + len(inputs): 0},
        compiler_params=params(LIMIT),
        cost_estimate=cost(6),
        name="mix",
    )(place, *[array for array, _, _ in inputs], resid)


def expert_kernel(
    per, place, merged, d_expert, w_in, w_out, out, d_merged, keep, give, acc, d_acc, rows_t
):
    step = pl.program_id(0)
    rows = merged[0]
    back = d_expert[0]
    width = back.shape[1]
    root = math.sqrt(2.0 / math.pi)
    parts = w_in.shape[2] // TILE
    many = width // per
    mine = place[2] == 0

    @pl.when(step == 0)
    def _():
        rows_t[...] = rows.T

    def spans(n):
        return slice(n * TILE, (n + 1) * TILE)

    def ahead(n):
        return dot(rows, w_in[0, :, spans(n)]), dot_nt(back, w_out[0, spans(n), :])

    def bend(u, d_hidden):
        square = u * u
        bent = jnp.tanh(u * (root + (root * 0.044715) * square))
        hidden = (0.5 * u * (1.0 + bent)).astype(BF)
        slope = 0.5 * (1.0 + bent) + (0.5 * u) * (1.0 - bent * bent) * (
            root + (3.0 * root * 0.044715) * square
        )
        return hidden, (d_hidden * slope).astype(BF)

    def spread(n, hidden, d_pre):
        to_out = dot(hidden.T, back)
        to_out = jnp.concatenate([to_out[:, :TILE], to_out[:, TILE:]], axis=0)
        to_in = dot(rows_t[...], d_pre)
        shape = (many, per, TILE)
        at = slice(n * many, (n + 1) * many)
        keep[at] = jnp.where(mine, to_in, to_out).astype(BF).reshape(shape)
        give[at] = jnp.where(mine, to_out, to_in).astype(BF).reshape(shape)
        return dot(hidden, w_out[0, spans(n), :]), dot_nt(d_pre, w_in[0, :, spans(n)])

    forth, down, waiting = 0.0, 0.0, None
    current = ahead(0)
    for n in range(parts):
        later = ahead(n + 1) if n + 1 < parts else None
        bent = bend(*current)
        if waiting is not None:
            pair = spread(*waiting)
            forth, down = forth + pair[0], down + pair[1]
        waiting = (n,) + bent
        current = later
    pair = spread(*waiting)
    forth, down = forth + pair[0], down + pair[1]

    @pl.when(step == 0)
    def _():
        acc[...] = forth
        d_acc[...] = down

    @pl.when(step == pl.num_programs(0) - 1)
    def _():
        out[...] = (acc[...] + forth).astype(BF)
        d_merged[...] = (d_acc[...] + down).astype(BF)


def expert(e, place, count, merged, d_expert, w_in, w_out, deps):
    _, rows, width = merged.shape
    hidden = w_in.shape[2]
    chunk = hidden // 2
    per = hidden // TILE * width // count
    one = ((1, rows, width), same(e, 0, 0))
    flat = ((rows, width), BF, (rows, width), same(0, 0))
    part = ((count, per, TILE), BF, (count // 2, per, TILE), lambda f, s: (f, 0, 0))
    return call(
        lambda *refs: expert_kernel(per, *refs),
        "expert",
        13,
        (2,),
        [
            (merged, *one),
            (d_expert, *one),
            (w_in, (1, width, chunk), lambda f, s: (e, 0, f)),
            (w_out, (1, chunk, width), lambda f, s: (e, f, 0)),
        ],
        [flat, flat, part, part],
        [
            pltpu.VMEM((rows, width), F32),
            pltpu.VMEM((rows, width), F32),
            pltpu.VMEM((width, rows), BF),
        ],
        deps,
        place,
    )


def low_kernel(
    place, resid, cot, gates, x0, x1, m0, m1, router, gain, d2, d3, d0, lows_out, g_router, g_gain
):
    slots, rows, width = resid.shape
    outs = [x0[...].astype(F32), x1[...].astype(F32)]
    downs = [m0[...].astype(F32), m1[...].astype(F32)]
    lane = lax.broadcasted_iota(jnp.int32, (rows, 128), 1)
    hats, inverses, seconds, d_gates = [], [], [], []
    for r in range(slots):
        slot = lax.rem(r + 2 * place[0], slots)
        hat, inverse = normed(resid[r])
        second = (hat * gain[...]).astype(BF)
        hats.append(hat)
        inverses.append(inverse)
        seconds.append(second)
        cotangent = cot[slot].astype(F32)
        second = second.astype(F32)
        columns = [
            jnp.sum(cotangent * outs[e] + downs[e] * second, axis=-1, keepdims=True)
            for e in range(2)
        ]
        d_gates.append(jnp.where(lane == 0, columns[0], jnp.where(lane == 1, columns[1], 0.0)))
    mean = sum(gates[r] * d_gates[r] for r in range(slots))
    lows = [(gates[r] * (d_gates[r] - mean)).astype(BF) for r in range(slots)]
    gain_sum = jnp.zeros((1, width), F32)
    for r in range(slots):
        low = lows[r].astype(F32)
        lows_out[r] = low
        if r != 1:
            d_rows, gain_part = resid_back(
                cot[lax.rem(r + 2 * place[0], slots)], gates[r], low, downs, router, gain,
                hats[r], inverses[r],
            )
            {2: d2, 3: d3, 0: d0}[r][...] = d_rows
            gain_sum = gain_sum + gain_part
    low_rows = jnp.concatenate(lows, axis=0).astype(F32).T[:8].astype(BF)
    router_sum = dot(low_rows, jnp.concatenate(seconds, axis=0))
    add_up(g_router, router_sum)
    add_up(g_gain, jnp.broadcast_to(gain_sum, (8, width)))


def add_up(ref, value):
    @pl.when(pl.program_id(0) == 0)
    def _():
        ref[...] = value

    @pl.when(pl.program_id(0) > 0)
    def _():
        ref[...] += value


def resid_back(cotangent, gate, low, downs, router, gain, hat, inverse):
    weight = gate.astype(BF).astype(F32)
    d_second = sum(
        weight[:, e : e + 1] * downs[e] + low[:, e : e + 1] * router[e : e + 1, :]
        for e in range(2)
    )
    d_stream = norm_back(d_second * gain[...], hat, inverse)
    d_rows = (cotangent.astype(F32) + d_stream).astype(BF)
    return d_rows, jnp.sum(d_second * hat, axis=0, keepdims=True)


def own_kernel(
    place, resid, cot, gates, lows, m0, m1, router, gain, c0, c1, c2, c3, d0, d2, d3, g_router,
    g_gain_far, d1, keep, give, g_gain, g_out,
):
    step = pl.program_id(0)
    width = resid.shape[2]
    downs = [m0[...].astype(F32), m1[...].astype(F32)]
    hat, inverse = normed(resid[0])
    d_rows, gain_part = resid_back(
        cot[0], gates[0], lows[0], downs, router, gain, hat, inverse
    )
    d1[...] = d_rows
    add_up(g_gain, jnp.broadcast_to(gain_part, (8, width)))
    cores = jnp.concatenate([c0[...], c1[...], c2[...], c3[...]], axis=0)
    rows = jnp.concatenate([d0[...], d_rows, d2[...], d3[...]], axis=0)
    total = dot(cores.T, rows)

    add_up(g_out, total)

    @pl.when(step == pl.num_programs(0) - 1)
    def _():
        mine = place[2] == 0
        low, high = g_out[:, :TILE], g_out[:, TILE:]
        line = lax.broadcasted_iota(jnp.int32, (8, width), 0)
        small = jnp.where(line < 2, g_router[...], 0.0)
        small = jnp.where(line == 2, g_gain_far[...] + g_gain[...], small)
        small = jnp.concatenate(
            [small[:, :TILE], small[:, TILE:], jnp.zeros((width - 16, TILE), F32)], axis=0
        )
        blank = jnp.zeros((width, TILE), F32)
        one = jnp.concatenate([jnp.where(mine, low, high), jnp.where(mine, small, blank)])
        two = jnp.concatenate([jnp.where(mine, high, low), jnp.where(mine, blank, small)])
        keep[...] = one.astype(BF)
        give[...] = two.astype(BF)


def output_kernel(place, resid, gates, x0, x1, output):
    slots = resid.shape[0]
    outs = [x0[...].astype(F32), x1[...].astype(F32)]
    for r in range(slots):
        slot = lax.rem(r + 2 * place[0], slots)
        weight = gates[r].astype(BF).astype(F32)
        output[slot] = (
            resid[r] + weight[:, 0:1] * outs[0] + weight[:, 1:2] * outs[1]
        ).astype(BF)


def blocks_of(slots, rows, width):
    return dict(
        quad=((slots, rows, width), lambda p, s: (0, p, 0)),
        other=((1, rows, width), lambda p, s: (1, p, 0)),
        our_other=((1, rows, width), lambda p, s: (2 * s[0] + 1, p, 0)),
        other_lanes=((1, rows, 128), lambda p, s: (1, p, 0)),
        lanes=((slots, rows, 128), lambda p, s: (0, p, 0)),
        part=((rows, width), lambda p, s: (p, 0)),
        eight=((8, width), same(0, 0)),
    )


def unmix_far(place, resid, cotangent, gates, outs, downs, router, gain, deps):
    slots, half, width = resid.shape
    b = blocks_of(slots, 256, width)
    return call(
        low_kernel,
        "unmix_far",
        9,
        (half // 256,),
        [(resid, *b["quad"]), (cotangent, *b["quad"]), (gates, *b["lanes"])]
        + [(value, *b["part"]) for value in (*outs, *downs)]
        + [whole(router), whole(gain)],
        [((half, width), BF, *b["part"])] * 3
        + [((slots, half, 128), F32, *b["lanes"])]
        + [((8, width), F32, *b["eight"])] * 2,
        [],
        deps,
        place,
    )


def unmix_own(
    place, resid, cotangent, gates, lows, downs, router, gain, cores, d_rows, g_router, gain_far, deps
):
    slots, half, width = resid.shape
    b = blocks_of(slots, 256, width)
    rest = ((2 * width, TILE), BF, (2 * width, TILE), same(0, 0))
    return call(
        own_kernel,
        "unmix_own",
        1,
        (half // 256,),
        [(resid, *b["other"]), (cotangent, *b["our_other"])]
        + [(value, *b["other_lanes"]) for value in (gates, lows)]
        + [(value, *b["part"]) for value in downs]
        + [whole(router), whole(gain)]
        + [(value, *b["part"]) for value in (*cores, *d_rows)]
        + [whole(g_router), whole(gain_far)],
        [((half, width), BF, *b["part"]), rest, rest],
        [pltpu.VMEM((8, width), F32), pltpu.VMEM((width, width), F32)],
        deps,
        place,
    )


def write_output(place, resid, gates, outs, deps):
    slots, half, width = resid.shape
    b = blocks_of(slots, 128, width)
    return call(
        output_kernel,
        "write_output",
        1,
        (half // 128,),
        [(resid, *b["quad"]), (gates, *b["lanes"])] + [(value, *b["part"]) for value in outs],
        [((slots, half, width), BF, *b["quad"])],
        [],
        deps,
        place,
    )[0]


def backward_kernel(
    place, d_own, d_got, query, keys, values, core_own, core_far, stats, wo, three,
    d_attn, core, dq_t, d_keys, d_values,
):
    half = d_own.shape[0]
    full = 2 * half
    here = pl.multiple_of(place[0] * half, half)
    there = pl.multiple_of((1 - place[0]) * half, half)
    d_attn[pl.ds(here, half), :] = d_own[...]
    d_attn[pl.ds(there, half), :] = d_got[...]
    core[pl.ds(here, half), :] = core_own[...]
    core[pl.ds(there, half), :] = core_far[...]
    d_core = dot_nt(d_attn[...], wo[...]).astype(BF)
    product = (d_core.astype(F32) * core[...].astype(F32)).T
    masks = lane_masks(BF)
    keys_t = keys[...].T
    causal = causal_tile()
    tasks = [
        (head, block) for head in range(query.shape[1] // HEAD) for block in range(full // TILE)
    ]

    def of_pair(head):
        return slice(head // 2 * PAIR, (head // 2 + 1) * PAIR)

    def score(head, block):
        pair, mask, count = of_pair(head), masks[head % 2], (block + 1) * TILE
        span = slice(block * TILE, count)
        scores = dot_nt(keys[:count, pair] * mask, query[span, pair])
        d_probs = dot_nt(values[:count, pair] * mask, d_core[span, pair])
        return scores, d_probs

    def soften(head, block, scores, d_probs):
        count = (block + 1) * TILE
        span = slice(block * TILE, count)
        delta = jnp.sum(product[head * HEAD : (head + 1) * HEAD, span], axis=0, keepdims=True)
        probs = jnp.exp2(scores * SCALE2 - stats[0, head : head + 1, span])
        near = jnp.where(causal, probs[count - TILE :], 0.0)
        if block > 0:
            near = jnp.concatenate([probs[: count - TILE], near], axis=0)
        return near.astype(BF), (near * (d_probs - delta)).astype(BF)

    def spread(head, block, probs, d_scores):
        pair, mask, count = of_pair(head), masks[head % 2], (block + 1) * TILE
        span, before = slice(block * TILE, count), slice(0, count - TILE)
        lanes = slice(head * HEAD, (head + 1) * HEAD)
        to_value = dot(probs, d_core[span, pair] * mask)
        to_key = dot(d_scores, query[span, pair] * mask)
        if head % 2 == 0:
            d_values[span, pair] = to_value[count - TILE :]
            d_keys[span, pair] = to_key[count - TILE :]
            if block > 0:
                d_values[before, pair] += to_value[before]
                d_keys[before, pair] += to_key[before]
        else:
            d_values[:count, pair] += to_value
            d_keys[:count, pair] += to_key
        dq_t[lanes, span] = dot(keys_t[lanes, :count], d_scores)

    scored = score(*tasks[0])
    waiting = None
    for n, task in enumerate(tasks):
        ahead = score(*tasks[n + 1]) if n + 1 < len(tasks) else None
        softened = soften(*task, *scored)
        if waiting is not None:
            spread(*waiting)
        waiting = task + softened
        scored = ahead
    spread(*waiting)
    three[:, :QUAD] = (dq_t[...].T * SCALE).astype(BF)
    three[:, QUAD : 2 * QUAD] = (d_keys[...] * SCALE).astype(BF)
    three[:, 2 * QUAD :] = d_values[...].astype(BF)


def attend_back(us, quads, place, d_own, d_got, kept, wo, deps):
    first, query, keys, values, core_own, core_far, stats = kept
    half, width = d_own.shape
    full = 2 * half
    start, count = quads

    def column(rows):
        return (rows, QUAD), lambda p, s: (0, start + p)

    return call(
        backward_kernel,
        "attend_backward",
        us,
        (count,),
        [
            whole(d_own),
            whole(d_got),
            (query, *column(full)),
            (keys, *column(full)),
            (values, *column(full)),
            (core_own, *column(half)),
            (core_far, *column(half)),
            (stats, (1, 8, full), lambda p, s: (start + p, 0, 0)),
            (wo, (QUAD, width), lambda p, s: (start + p, 0)),
        ],
        [((full, count * 3 * QUAD), BF, (full, 3 * QUAD), lambda p, s: (0, p))],
        [
            pltpu.VMEM((full, width), BF),
            pltpu.VMEM((full, QUAD), BF),
            pltpu.VMEM((QUAD, full), F32),
            pltpu.VMEM((full, QUAD), F32),
            pltpu.VMEM((full, QUAD), F32),
        ],
        deps,
        place,
    )[0]


def first_kernel(place, t0, t1, own, got, gain, wq, wk, wv, d_tok_own, d_tok_far):
    d_first = 0.0
    for quad, three in enumerate((t0, t1)):
        lanes = slice(quad * QUAD, (quad + 1) * QUAD)
        weights = [w[:, lanes] for w in (wq, wk, wv)]
        d_first = d_first + dot_nt(three[...], jnp.concatenate(weights, axis=1))
    near = pl.program_id(0) == 0
    value = jnp.where(near, own[0].astype(F32), got[...].astype(F32))
    hat, inverse = normed(value)
    result = norm_back(d_first * gain[...], hat, inverse).astype(BF)

    @pl.when(near)
    def _():
        d_tok_own[...] = result

    @pl.when(jnp.logical_not(near))
    def _():
        d_tok_far[...] = result


def first_back(us, index, place, threes, tokens, got, gain, weights, deps):
    _, half, width = tokens.shape
    rows = 256
    blocks = half // rows

    def row_block(h, j, s):
        return jnp.where(h == 0, s[0], 1 - s[0]) * blocks + j

    return call(
        first_kernel,
        "first_back",
        us,
        (2, blocks),
        [
            (three, (rows, 3 * QUAD), lambda h, j, s, c=c: (row_block(h, j, s), c))
            for three, c in threes
        ]
        + [
            (
                tokens,
                (1, rows, width),
                lambda h, j, s: (2 * s[0] + index, jnp.where(h == 0, j, blocks - 1), 0),
            ),
            (got, (rows, width), lambda h, j, s: (jnp.where(h == 0, 0, j), 0)),
            whole(gain),
            *[whole(weight) for weight in weights],
        ],
        [
            (
                (half, width),
                BF,
                (rows, width),
                lambda h, j, s: (jnp.where(h == 0, j, blocks - 1), 0),
            ),
            ((half, width), BF, (rows, width), lambda h, j, s: (jnp.where(h == 0, 0, j), 0)),
        ],
        [],
        deps,
        place,
    )


def token_kernel(place, *refs):
    slots = len(refs) // 2
    grad = refs[-1]
    for r in range(slots):
        slot = lax.rem(r + 2 * place[0], slots)
        grad[slot] = (refs[r][...].astype(F32) + refs[slots + r][...].astype(F32)).astype(BF)


def token_grads(place, d_rows, t_rows, shape, deps):
    slots, half, width = shape
    b = blocks_of(slots, 128, width)
    return call(
        token_kernel,
        "token_grads",
        4,
        (half // 128,),
        [(value, *b["part"]) for value in (*d_rows, *t_rows)],
        [(shape, BF, *b["quad"])],
        [],
        deps,
        place,
    )[0]


def early_project_kernel(place, first, low_three, high_three, low, high):
    low[...] = dot_tn(first[...], low_three[...])
    high[...] = dot_tn(first[...], high_three[...])


def project_kernel(place, first, low_three, high_three, low, high, keep, give):
    mine = place[2] == 0
    low_sum = low[...] + dot_tn(first[...], low_three[...])
    high_sum = high[...] + dot_tn(first[...], high_three[...])
    keep[...] = jnp.where(mine, low_sum, high_sum).astype(BF)
    give[...] = jnp.where(mine, high_sum, low_sum).astype(BF)


def project_grads(place, first, threes, earlier, deps):
    full, width = first.shape
    block = ((width, QUAD), lambda p, s: (p, 0))
    out = ((3 * width, QUAD), BF if earlier else F32, *block)
    return call(
        project_kernel if earlier else early_project_kernel,
        "project_grads",
        1,
        (3,),
        [whole(first)]
        + [(three, (full, QUAD), lambda p, s, c=c: (0, 3 * c + p)) for three, c in threes]
        + [(value, *block) for value in earlier],
        [out, out],
        [],
        deps,
        place,
    )


def chip_bits(devices):
    return [1] + [1 << n for n in range(2, devices.bit_length() - 1)]


def masks_of(level):
    return [level[0], level[1], level[0] + level[1]] if len(level) > 1 else [level[0]]


def send(value, mask, devices):
    return lax.ppermute(value, AXES, [(n, n ^ mask) for n in range(devices)])


class Summed:
    def __init__(self, lanes, devices, levels, lane_levels):
        self.devices, self.levels, self.lane_levels = devices, levels, lane_levels
        self.steps, self.count, self.parts = 0, len(levels), None
        self.arrays, self.orders, self.rows = [], [], []
        for lane, own in zip(lanes, lane_levels):
            self.arrays += [[keep, send(give, 2, devices)] for keep, give in lane]
            order = own[0] if len(own) == 1 else [bit for level in reversed(own) for bit in level]
            self.orders += [order] * len(lane)
            self.rows.append(sum(keep.shape[1] for keep, _ in lane))

    def jobs(self):
        n = self.steps
        if n == 0:
            return [(self.arrays, self.levels[0], self.orders)]
        if n <= self.count:
            level = self.levels[n] if n < self.count else []
            return [(self.arrays, level, [level] * len(self.arrays))]
        if self.parts is not None:
            return [(part, None, [part[0][0].shape[1]]) for part in self.parts]
        return [(self.arrays, None, self.rows if n == 2 * self.count - 1 else [sum(self.rows)])]

    def take(self, results):
        n, count = self.steps, self.count
        self.steps += 1
        if n < count:
            mine, *others = results[0]
            masks = masks_of(self.levels[n])
            got = [send(other, mask, self.devices) for other, mask in zip(others, masks)]
            self.arrays = [[mine] + got]
            return
        values = [value for result in results for value in result]
        if n < 2 * count - 1:
            masks = masks_of(self.levels[2 * count - 1 - n])
            self.arrays = [values + [send(values[0], mask, self.devices) for mask in masks]]
            return
        self.parts = []
        for own, value in zip(self.lane_levels, values):
            masks = masks_of(own[len(own) - 1 - (n - 2 * count + 1)])
            self.parts.append([[value] + [send(value, mask, self.devices) for mask in masks]])

    def done(self):
        return self.steps >= 2 * self.count - 1 + len(self.lane_levels[0])

    def exchange(self):
        self.early = [send(part[0][0], 2, self.devices) for part in self.parts]
        return self.early

    def finish(self):
        return [
            part[0] + [first] + [send(some, 2, self.devices) for some in part[0][1:]]
            for part, first in zip(self.parts, self.early)
        ]


def step_kernel(kinds, place, *refs):
    ins = sum(sum(groups) for _, groups, _ in kinds)
    inputs, outputs = refs[:ins], refs[ins:]
    for adds, groups, n_out in kinds:
        here, inputs = inputs[: sum(groups)], inputs[sum(groups) :]
        there, outputs = outputs[:n_out], outputs[n_out:]
        if not adds:
            size, row = here[0].shape[0], 0
            for target in there:
                rows = target.shape[1]
                for n, ref in enumerate(here):
                    target[n * size : (n + 1) * size] = ref[:, row : row + rows, :]
                row += rows
            continue
        for target in there:
            row = 0
            for each in groups[: len(groups) // n_out]:
                total = here[0][...].astype(F32)
                for other in here[1:each]:
                    total = total + other[...].astype(F32)
                here, rows = here[each:], total.shape[1]
                target[:, row : row + rows, :] = total.astype(BF)
                row += rows


def advance(chains, place, deps, us=3):
    jobs = [chain.jobs() for chain in chains]
    every = [job for some in jobs for job in some]
    splits = [arrays[0][0].shape[0] >> len(level or []) for arrays, level, _ in every]
    big = max(array[0].size for arrays, _, _ in every for array in arrays)
    steps = max(1, 4 * big // MIB) if all(level is not None for _, level, _ in every) else 1
    steps = min([steps] + splits)
    inputs, outputs, kinds = [], [], []
    for (arrays, level, orders), split in zip(every, splits):
        width = arrays[0][0].shape[2]
        if level is None:
            count = split * len(arrays[0])
            inputs += [whole(array) for array in arrays[0]]
            for rows in orders:
                shape = (count, rows, width)
                outputs.append((shape, BF, shape, lambda p, s: (0, 0, 0)))
            kinds.append((False, [len(arrays[0])], len(orders)))
            continue
        block = split // steps
        rows = sum(some[0].shape[1] for some in arrays)

        def index(mask, order):
            def at(p, s):
                own = 0
                for n, bit in enumerate(order):
                    own = own + (lax.rem(s[4] // bit + (1 if mask & bit else 0), 2) << n)
                return (own * steps + p, 0, 0)

            return at

        for mask in [0] + (masks_of(level) if level else []):
            for some, order in zip(arrays, orders):
                inputs += [(a, (block,) + a.shape[1:], index(mask, order)) for a in some]
            outputs.append(
                ((split, rows, width), BF, (block, rows, width), lambda p, s: (p, 0, 0))
            )
        n_out = 1 << len(level)
        kinds.append((True, [len(some) for some in arrays] * n_out, n_out))
    results = call(
        lambda *refs: step_kernel(kinds, *refs), "sum_step", us, (steps,), inputs, outputs, [],
        deps, place,
    )
    mark, groups = results[0], []
    for _, _, n_out in kinds:
        groups.append(results[:n_out])
        results = results[n_out:]
    for chain, some in zip(chains, jobs):
        chain.take(groups[: len(some)])
        groups = groups[len(some) :]
    return [mark]


def result_kernel(per, each, experts, place, *refs):
    held, (grad_in, grad_out) = refs[:-2], refs[-2:]
    mine = place[2] == 0
    half = each // 2
    for n, e in enumerate(experts):

        @pl.when(pl.program_id(0) == n)
        def _():
            own, other = held[2 * n : 2 * n + 2]
            swap = place[3 + 2 * e] & (each - 1)
            for t in range(each):
                first, second = own[t ^ swap].astype(F32), other[t ^ swap].astype(F32)
                low, high = jnp.where(mine, first, second), jnp.where(mine, second, first)
                grad_in[0, t * per : (t + 1) * per, :] = low
                lanes = slice(t // half * TILE, (t // half + 1) * TILE)
                grad_out[0, t % half * per : (t % half + 1) * per, lanes] = high


def expert_results(experts, d, place, parts, width, hidden, per, earlier, deps):
    inner = parts[0][0].shape[0]
    each = width // per
    blocks = inner // each

    def chip(e, s):
        return s[3 + 2 * e]

    def expert(n):
        return n + experts[0]

    def piece(n, k, s):
        some = jnp.where(expert(n) == 0, s[3], s[5])
        return (d ^ (some // inner)) * blocks + k

    def part_index(own):
        def index(n, k, s):
            e, first = expert(n), (chip(own, s) % inner) // each
            at = jnp.where(e == own, k, jnp.where(e < own, 0, blocks - 1))
            return (at ^ first, 0, 0)

        return index

    inputs = []
    for e in experts:
        inputs += [
            (parts[e][n], (each, per, TILE), part_index(e)) for n in (d, len(parts[e]) // 2 + d)
        ]
    outputs = [
        ((2, width, hidden), F32, (1, width, TILE), lambda n, k, s: (expert(n), 0, piece(n, k, s))),
        ((2, hidden, width), F32, (1, TILE, width), lambda n, k, s: (expert(n), piece(n, k, s), 0)),
    ]
    any_ref = pl.BlockSpec(memory_space=pl.ANY)
    held = len(earlier) + len(deps)

    def body(place_ref, *refs):
        result_kernel(per, each, experts, place_ref, *refs[held:])

    return pl.pallas_call(
        body,
        grid_spec=pltpu.PrefetchScalarGridSpec(
            num_scalar_prefetch=1,
            grid=(len(experts), blocks),
            in_specs=[any_ref] * held + [pl.BlockSpec(b, i) for _, b, i in inputs],
            out_specs=[pl.BlockSpec(b, i) for _, _, b, i in outputs],
        ),
        out_shape=[jax.ShapeDtypeStruct(shape, kind) for shape, kind, _, _ in outputs],
        input_output_aliases={1 + n: n for n in range(len(earlier))},
        compiler_params=params(LIMIT, "arbitrary", "arbitrary"),
        cost_estimate=cost(5 * len(experts)),
        name="expert_results",
    )(place, *earlier, *deps, *[array for array, _, _ in inputs])


def project_result_kernel(place, *refs):
    count = (len(refs) - 13) // 2
    parts, others = refs[:count], refs[count : 2 * count]
    weights, gain = refs[2 * count : 2 * count + 3], refs[2 * count + 3]
    grads = refs[2 * count + 4 : 2 * count + 8]
    g_gain, g_gain2, g_router, halves, rest = refs[2 * count + 8 :]
    inner, rows, _ = parts[0].shape
    width = gain.shape[1]
    per = 3 * width // (count * inner)
    for d in range(count):
        for m in range(inner):
            shard = (d * inner + m) ^ place[3]
            at = pl.ds(pl.multiple_of(shard * per, 8), per)
            more = pl.ds(pl.multiple_of(shard * (rows - per), 8), rows - per)
            for half, source in ((place[2], parts), (1 - place[2], others)):
                value = source[d][m].astype(F32)
                halves[half, at, :] = value[:per]
                rest[half, more, :] = value[per:]
    total = jnp.zeros((width, 1), F32)
    for n in range(4):
        for h in range(2):
            lanes = slice(h * QUAD, (h + 1) * QUAD)
            if n == 3:
                grads[n][:, lanes] = rest[h, :width, :]
                continue
            value = halves[h, n * width : (n + 1) * width, :]
            grads[n][:, lanes] = value
            total += jnp.sum(value * weights[n][:, lanes].astype(F32), axis=1, keepdims=True)
    g_gain[...] = jnp.broadcast_to(total, (width, 128)).T[:1] / gain[...]
    for h in range(2):
        lanes = slice(h * QUAD, (h + 1) * QUAD)
        small = rest[0, width + 8 * h : width + 8 * (h + 1), :]
        g_router[:, lanes] = small[:2]
        g_gain2[:, lanes] = small[2:3]


def project_result(place, chip, parts, weights, gain, deps):
    width = gain.shape[1]
    square = ((width, width), F32, (width, width), same(0, 0))
    line = ((1, width), F32, (1, width), same(0, 0))
    return call(
        project_result_kernel,
        "project_result",
        1,
        (1,),
        [whole(value) for value in (*parts, *weights, gain)],
        [square] * 4 + [line, line, ((2, width), F32, (2, width), same(0, 0))],
        [pltpu.VMEM((2, 3 * width, QUAD), F32), pltpu.VMEM((2, 2 * width, QUAD), F32)],
        deps,
        place.at[3].set(chip),
    )


def shards(
    tokens, seq_counts, norm1_gain, w_query, w_key, w_value, output_weight, norm2_gain,
    router_weight, w_expert_in, w_expert_out, cotangent,
):
    slots, half, width = tokens.shape
    hidden = w_expert_in.shape[2]
    devices = lax.axis_size("dp") * lax.axis_size("blk")
    count = devices // 2
    blk = lax.axis_index("blk")
    dp = lax.axis_index("dp")
    me = dp * 2 + blk
    core_bit = lax.rem(dp, 2)
    bits = chip_bits(devices)
    x, y, *more = bits
    levels = [bits[n : n + 2] for n in range(0, len(bits), 2)]
    lanes = [[[y], [x]], [[x], [y]]]

    def chip_of(levels):
        chip = jnp.int32(0)
        for level in levels:
            for bit in reversed(level):
                chip = chip * 2 + lax.rem(me // bit, 2)
        return chip

    place = jnp.stack([blk, seq_counts[0], core_bit, jnp.int32(0), me]).astype(jnp.int32)
    gain1 = norm1_gain.reshape(1, width)
    gain2 = norm2_gain.reshape(1, width)
    router = jnp.pad(router_weight, ((0, 0), (0, 126)))
    router_rows = jnp.pad(router_weight.T.astype(F32), ((0, 6), (0, 0)))
    weights = (w_query, w_key, w_value)

    def swap(value):
        return send(value, 1, devices)

    far = [
        lax.dynamic_index_in_dim(tokens, lax.rem(2 + i + 2 * blk, 4), 0, keepdims=False)
        for i in range(2)
    ]
    got = [swap(value) for value in far]
    kept = [
        attend(i, place, tokens, got[i], gain1, w_query, w_key, w_value) for i in range(2)
    ]
    cores = [kept[0][4], kept[1][4], swap(kept[0][5]), swap(kept[1][5])]
    early = mix_early(place, tokens, cores[:3], output_weight, gain2, router)
    resid, merged, d_expert, gates = mix(
        place, tokens, cotangent, cores[3], early, output_weight, gain2, router
    )
    per = hidden // TILE * width // count
    done = [expert(0, place, count, merged, d_expert, w_expert_in, w_expert_out, [])]
    done.append(
        expert(1, place, count, merged, d_expert, w_expert_in, w_expert_out, [done[0][0]])
    )
    outs, downs = [d[0] for d in done], [d[1] for d in done]
    summed = Summed([[done[0][2:4]], [done[1][2:4]]], devices, levels, lanes)
    d2, d3, d0, lows, g_router, gain_far = unmix_far(
        place, resid, cotangent, gates, outs, downs, router_rows, gain2, []
    )
    d_got = [swap(d2), swap(d3)]
    marks = advance([summed], place, [d2])

    a0 = attend_back(15, (0, 1), place, d0, d_got[0], kept[0], output_weight, marks)
    a1 = attend_back(15, (1, 1), place, d0, d_got[0], kept[0], output_weight, [a0])
    d1, *rest = unmix_own(
        place, resid, cotangent, gates, lows, downs, router_rows, gain2, cores, [d0, d2, d3],
        g_router, gain_far, [a1],
    )
    rest = [value.reshape(count, -1, TILE) for value in rest]
    threes = [[(a0, 0), (a1, 0)]]
    far_a = first_back(1, 0, place, threes[0], tokens, got[0], gain1, weights, [d1, d_got[1]])
    t_far = [swap(far_a[1])]

    def back(quad, us, deps):
        return attend_back(us, (quad, 1), place, d1, d_got[1], kept[1], output_weight, deps)

    b0 = back(0, 1, [far_a[0]])
    early = project_grads(place, kept[0][0], threes[0], [], [b0])
    b1 = back(1, 20, [t_far[0]] + advance([summed], place, [early[0]]))
    threes.append([(b0, 0), (b1, 0)])
    pair = project_grads(place, kept[1][0], threes[1], early, [b1])
    pair = [value.reshape(count, -1, QUAD) for value in pair]
    last = Summed([[pair, rest]], devices, levels, [levels[:1]])
    marks = advance([summed], place, [pair[0]])
    marks = advance([last], place, marks)
    far_b = first_back(6, 1, place, threes[1], tokens, got[1], gain1, weights, marks)
    t_far.append(swap(far_b[1]))
    marks = advance([summed, last], place, [far_b[0]])
    output = write_output(place, resid, gates, outs, marks)
    marks = advance([last], place, [output], 1)
    while not summed.done():
        marks = advance([summed], place, marks + [t_far[1]], 1)
    grad_tokens = token_grads(
        place, (d0, d1, d2, d3), (far_a[0], far_b[0], *t_far), (slots, half, width), marks
    )
    marks = marks + summed.exchange() + [grad_tokens]
    while not last.done():
        marks = advance([last], place, marks, 1)
    last.exchange()
    parts = summed.finish()
    chips = [chip_of(lane + levels[1:]) for lane in lanes]
    final = jnp.stack([blk, seq_counts[0], core_bit, chips[0], me, chips[1]]).astype(jnp.int32)
    results = []
    for e in range(2):
        results = expert_results((e,), 0, final, parts, width, hidden, per, results, [])
    grad_in, grad_out = expert_results(
        (0, 1), 1, final, parts, width, hidden, per, results, []
    )
    *grads, grad_gain1, grad_gain2, grad_router = project_result(
        place, chip_of(levels), last.finish()[0], weights, gain1, [grad_in]
    )
    return (
        output, grad_tokens, grad_gain1.reshape(width), *grads, grad_gain2.reshape(width),
        grad_router.T, grad_in, grad_out,
    )


def solution(mesh):
    data = P("dp", "blk", None)
    return jax.shard_map(
        shards,
        mesh=mesh,
        in_specs=(data, P("dp")) + (P(),) * 9 + (data,),
        out_specs=(data, data) + (P(),) * 9,
        check_vma=False,
    )
```
